128 devices in a mesh: dp: 4 (over x_hi, core), seq: 32 (over x_lo, y, z).
Axes of the slice: x: 4 (x_hi: 2, x_lo: 2; x = x_hi * 2 + x_lo), y: 4, z: 4, core: 2. Of those that a mesh axis runs over, the one named last changes fastest.
Arguments:
- hidden: bfloat16 [4, 4096, 2432], P('dp', 'seq'), may hold values from -6 to 6
- out_cot: bfloat16 [4, 4096, 2432], P('dp', 'seq'), may hold values from -6 to 6
- proj_in: bfloat16 [2432, 4096], P(None, 'dp'), may hold values from -0.125 to 0.125
- proj_out: bfloat16 [4096, 1536], P('dp'), may hold values from -0.09375 to 0.09375
- attn_out_w: bfloat16 [2048, 2432], replicated, may hold values from -0.125 to 0.125
- queries: bfloat16 [4, 4096, 2048], P('dp', 'seq'), as said below
- keys: bfloat16 [4, 4096, 2048], P('dp', 'seq'), as said below
- values: bfloat16 [4, 4096, 2048], P('dp', 'seq'), may hold values from -6 to 6
- dino: bfloat16 [4, 1536, 4096], P('dp', 'seq'), as said below
Outputs:
- cosine: float32 [4, 4096], P('dp', 'seq')
- grad_queries: bfloat16 [4, 4096, 2048], P('dp', 'seq')
- grad_keys: bfloat16 [4, 4096, 2048], P('dp', 'seq')
- grad_values: bfloat16 [4, 4096, 2048], P('dp', 'seq')
The draws below stay inside these ranges and needn't reach their ends.
Inputs may be any that keep to these rules, and one draw needn't show every extreme that they name: `dino`: real-valued features, channels of differing scale and offset. real-valued queries. real-valued keys.
All inputs are finite; a program needn't handle non-finite values.
Results may differ from the reference program's by a relative error of at most 0.014.
Values may be sent and summed in bfloat16 or wider, within the bound.
A program may use at most 128 MiB of HBM per device.

```python
import jax
import jax.numpy as jnp
from jax import lax

D = 2432
PROJ_HID = 4096
D_DINO = 1536
HEADS = 32
HEAD_DIM = 64
IMAGES = 4
TOKENS = 4096


def query_key_pair(key):
    shape = (IMAGES, TOKENS, HEADS * HEAD_DIM)
    base = jax.random.fold_in(key, 4711)
    key_query, key_keys = jax.random.split(base, 2)
    query_draw = jax.random.truncated_normal(key_query, -4.0, 4.0, shape, jnp.float32)
    key_draw = jax.random.truncated_normal(key_keys, -4.0, 4.0, shape, jnp.float32)
    return (query_draw, key_draw)


def draw_queries(key, part):
    return query_key_pair(key)[0].astype(jnp.bfloat16)


def draw_keys(key, part):
    return query_key_pair(key)[1].astype(jnp.bfloat16)


def draw_dino(key, part):
    key_base, key_scale, key_shift = jax.random.split(jax.random.fold_in(key, 911), 3)
    base = jax.random.normal(key_base, (IMAGES, D_DINO, TOKENS), jnp.float32)
    channel_scale = jnp.exp(jax.random.uniform(key_scale, (1, D_DINO, 1), jnp.float32, 0.0, 2.302585))
    channel_shift = 2.0 * jax.random.normal(key_shift, (1, D_DINO, 1), jnp.float32)
    features = base * channel_scale + channel_shift
    return features.astype(jnp.bfloat16)


def block_scale(key, dims, pieces, low, largest):
    factor_of, own = 1.0, jax.random.fold_in(key, 6)
    for axis_at, blocks in pieces:
        steps = jnp.exp(jax.random.uniform(jax.random.fold_in(own, axis_at), (blocks,), jnp.float32, low / len(pieces), largest / len(pieces)))
        factor_of = factor_of * jnp.repeat(steps, dims[axis_at] // blocks).reshape([-1 if axis == axis_at else 1 for axis in range(len(dims))])
    return factor_of


def scatter_about(rng, extent, scale, most, shards=(), held_as=jnp.bfloat16):
    gain = block_scale(rng, extent, shards, -0.22, 0.18) if shards else 1.0
    entries = jax.random.normal(rng, extent, jnp.float32) * scale * gain
    return jnp.minimum(jnp.maximum(entries, -most), most).astype(held_as)


def setup_inputs(seed: int = 0) -> dict:
    arg_keys = jax.random.split(jax.random.key(seed), 10)
    hidden = scatter_about(arg_keys[0], (IMAGES, TOKENS, D), 1.0, 6.0, ((0, 4), (1, 32)))
    out_cot = scatter_about(arg_keys[1], (IMAGES, TOKENS, D), 1.0, 6.0, ((0, 4), (1, 32)))
    proj_in = scatter_about(arg_keys[2], (D, PROJ_HID), D ** -0.5, 0.125, ((1, 4),))
    proj_out = scatter_about(arg_keys[3], (PROJ_HID, D_DINO), PROJ_HID ** -0.5, 0.09375, ((0, 4),))
    attn_out_w = scatter_about(arg_keys[4], (HEADS * HEAD_DIM, D), (HEADS * HEAD_DIM) ** -0.5, 0.125)
    queries = draw_queries(jax.random.fold_in(arg_keys[9], 71), 0)
    keys = draw_keys(jax.random.fold_in(arg_keys[9], 71), 0)
    values = scatter_about(arg_keys[7], (IMAGES, TOKENS, HEADS * HEAD_DIM), 1.0, 6.0, ((0, 4), (1, 32)))
    dino = draw_dino(jax.random.fold_in(arg_keys[9], 71), 0)
    return dict(hidden=hidden, out_cot=out_cot, proj_in=proj_in, proj_out=proj_out, attn_out_w=attn_out_w, queries=queries, keys=keys, values=values, dino=dino)


loss_weight = 1000.0

def unit_target(features):
    values32 = features.astype(jnp.float32)
    center = lax.optimization_barrier(jnp.mean(values32, axis=1, keepdims=True))
    shifted = values32 - center
    spread = lax.optimization_barrier(jnp.mean(shifted * shifted, axis=1, keepdims=True))
    normed = shifted * lax.rsqrt(spread + 1e-06)
    unit = normed * lax.rsqrt(lax.optimization_barrier(jnp.sum(normed * normed, axis=1, keepdims=True)) + 1e-06)
    return jnp.transpose(unit, (0, 2, 1))

def cosine_grad(projected, target):
    rinv = lax.rsqrt(lax.optimization_barrier(jnp.sum(projected * projected, axis=-1, keepdims=True)) + 1e-06)
    direction = projected * rinv
    cosine = lax.optimization_barrier(jnp.sum(direction * target, axis=-1))
    grad_z = -loss_weight * rinv * (target - cosine[..., None] * direction)
    return (cosine, grad_z.astype(jnp.bfloat16))

def silu_slope(pre_act):
    sigma = jax.nn.sigmoid(pre_act)
    return sigma * (1.0 + pre_act * (1.0 - sigma))

def head_backward(operands):
    query, key_rows, value_rows, grad_out = operands
    scale = HEAD_DIM ** (-0.5)
    scores = jnp.dot(query, key_rows.T, preferred_element_type=jnp.float32) * scale
    probs = jax.nn.softmax(scores, axis=-1)
    probs_b = probs.astype(jnp.bfloat16)
    attended = jnp.dot(probs_b, value_rows, preferred_element_type=jnp.float32)
    row_dot = lax.optimization_barrier(jnp.sum(grad_out.astype(jnp.float32) * attended, axis=-1, keepdims=True))
    grad_p = jnp.dot(grad_out, value_rows.T, preferred_element_type=jnp.float32)
    grad_s = (probs * (grad_p - row_dot)).astype(jnp.bfloat16)
    grad_q = (jnp.dot(grad_s, key_rows, preferred_element_type=jnp.float32) * scale).astype(jnp.bfloat16)
    grad_k = (jnp.dot(grad_s.T, query, preferred_element_type=jnp.float32) * scale).astype(jnp.bfloat16)
    grad_v = jnp.dot(probs_b.T, grad_out, preferred_element_type=jnp.float32).astype(jnp.bfloat16)
    return (grad_q, grad_k, grad_v)

def reference(hidden, out_cot, proj_in, proj_out, attn_out_w, queries, keys, values, dino):
    images = hidden.shape[0]
    length = hidden.shape[1]
    target = unit_target(dino).reshape(images * length, D_DINO)
    flat_hidden = hidden.reshape(images * length, D)
    pre_act = jnp.dot(flat_hidden, proj_in, preferred_element_type=jnp.float32)
    silu_out = jax.nn.silu(pre_act).astype(jnp.bfloat16)
    projected = jnp.dot(silu_out, proj_out, preferred_element_type=jnp.float32)
    cosine, grad_z = cosine_grad(projected, target)
    grad_silu = jnp.dot(grad_z, proj_out.T, preferred_element_type=jnp.float32)
    grad_pre = (grad_silu * silu_slope(pre_act)).astype(jnp.bfloat16)
    grad_repa = jnp.dot(grad_pre, proj_in.T, preferred_element_type=jnp.float32)
    grad_hidden = (out_cot.reshape(images * length, D).astype(jnp.float32) + grad_repa).astype(jnp.bfloat16)
    grad_attn = jnp.dot(grad_hidden, attn_out_w.T, preferred_element_type=jnp.float32).astype(jnp.bfloat16)

    def per_head(array):
        shaped = array.reshape(images, length, HEADS, HEAD_DIM)
        return jnp.transpose(shaped, (0, 2, 1, 3)).reshape(images * HEADS, length, HEAD_DIM)

    def back_layout(array):
        shaped = array.reshape(images, HEADS, length, HEAD_DIM)
        return jnp.transpose(shaped, (0, 2, 1, 3)).reshape(images, length, HEADS * HEAD_DIM)
    grad_q, grad_k, grad_v = lax.map(head_backward, (per_head(queries), per_head(keys), per_head(values), per_head(grad_attn)))
    return (cosine.reshape(images, length), back_layout(grad_q), back_layout(grad_k), back_layout(grad_v))
```

```python
from jax.sharding import PartitionSpec as P
import jax, jax.numpy as jnp
from jax import lax
from jax.experimental import pallas as pl
from jax.experimental.pallas import tpu as pltpu
LOG2E = 1.4426950408889634
F32=jnp.float32; BF=jnp.bfloat16
QB=512; KC=512; L=4096; NB=32; HD=64

def dot(a,b): return jnp.dot(a,b,preferred_element_type=F32)

def kern(q_ref,k_ref,v_ref,g_ref, dq_ref,dk_ref,dv_ref, kk,vv,kt,vt, s_ref,u_ref, ak,av):
    i = pl.program_id(0)
    per = QB//128
    @pl.when(i==0)
    def _():
        for j in range(NB):
            kb=k_ref[j]; vb=v_ref[j]
            rows=pl.ds(j*128,128)
            kn=kb.T; vn=vb.T
            kk[rows,:]=jnp.concatenate([kn,kn],axis=1)
            lane=lax.broadcasted_iota(jnp.int32,(128,HD),1)
            vv[rows,:]=jnp.concatenate([vn,jnp.where(lane<2,1.0,0.0).astype(BF)],axis=1)
            kt[:,rows]=kb*BF(0.125)
            vt[pl.ds(0,HD),rows]=vb
        vt[pl.ds(HD,16),:]=jnp.ones((16,L),BF)
        ak[...]=jnp.zeros_like(ak); av[...]=jnp.zeros_like(av)
    qt=jnp.concatenate([q_ref[i*per+j] for j in range(per)],axis=1)
    gt=jnp.concatenate([g_ref[i*per+j] for j in range(per)],axis=1)
    qf=qt.astype(F32)*(0.125*LOG2E)
    qhi=qf.astype(BF); qlo=(qf-qhi.astype(F32)).astype(BF)
    qa=jnp.concatenate([qhi,qlo],axis=0)
    m=jnp.full((8,QB),-jnp.inf,F32)
    for c in range(L//KC):
        rows=pl.ds(c*KC,KC)
        s=dot(kk[rows,:],qa)
        s_ref[rows,:]=s
        m=jnp.maximum(m,jnp.max(s.reshape(KC//8,8,QB),axis=0))
    m=jnp.max(m,axis=0,keepdims=True)
    acc=jnp.zeros((HD+16,QB),F32)
    for c in range(L//KC):
        rows=pl.ds(c*KC,KC)
        u=jnp.exp2(s_ref[rows,:]-m).astype(BF)
        u_ref[rows,:]=u
        acc=acc+dot(vt[:,rows],u)
    l=acc[HD:HD+1]
    rl=1.0/l
    gf=gt.astype(F32)
    d=-jnp.sum(gf*acc[:HD],axis=0,keepdims=True)*rl
    dhi=d.astype(BF); dlo=(d-dhi.astype(F32))
    row=lax.broadcasted_iota(jnp.int32,(HD,QB),0)
    tail=jnp.where(row==0,dhi.astype(F32),jnp.where(row==1,dlo,0.0)).astype(BF)
    ga=jnp.concatenate([gt,tail],axis=0)
    qn=(qt.astype(F32)*(rl*0.125)).T.astype(BF)
    gn=(gf*rl).T.astype(BF)
    dq=jnp.zeros((HD,QB),F32)
    for c in range(L//KC):
        rows=pl.ds(c*KC,KC)
        u=u_ref[rows,:]
        dp=dot(vv[rows,:],ga)
        ds=(u.astype(F32)*dp).astype(BF)
        ak[rows,:]+=dot(ds,qn)
        av[rows,:]+=dot(u,gn)
        dq=dq+dot(kt[:,rows],ds)
    dq=(dq*rl).astype(BF)
    for j in range(per):
        dq_ref[i*per+j]=dq[:,j*128:(j+1)*128]
    @pl.when(i==pl.num_programs(0)-1)
    def _():
        for j in range(NB):
            rows=pl.ds(j*128,128)
            dk_ref[j]=ak[rows,:].T.astype(BF)
            dv_ref[j]=av[rows,:].T.astype(BF)


def attention(q,k,v,g):
    full=pl.BlockSpec((NB,HD,128),lambda i:(0,0,0))
    return pl.pallas_call(kern,grid=(L//QB,),in_specs=[full]*4,out_specs=[full]*3,
        out_shape=[jax.ShapeDtypeStruct((NB,HD,128),BF)]*3,
        scratch_shapes=[pltpu.VMEM((L,128),BF),pltpu.VMEM((L,128),BF),pltpu.VMEM((HD,L),BF),pltpu.VMEM((HD+16,L),BF),
            pltpu.VMEM((L,QB),F32),pltpu.VMEM((L,QB),BF),pltpu.VMEM((L,HD),F32),pltpu.VMEM((L,HD),F32)],
        compiler_params=pltpu.CompilerParams(vmem_limit_bytes=56*2**20),name="attn")(q,k,v,g)


loss_weight = 1000.0


def unit_target(features):
    values32 = features.astype(jnp.float32)
    center = jnp.mean(values32, axis=1, keepdims=True)
    shifted = values32 - center
    spread = jnp.mean(shifted * shifted, axis=1, keepdims=True)
    normed = shifted * lax.rsqrt(spread + 1e-06)
    unit = normed * lax.rsqrt(jnp.sum(normed * normed, axis=1, keepdims=True) + 1e-06)
    return jnp.transpose(unit, (0, 2, 1))


def cosine_grad(projected, target):
    rinv = lax.rsqrt(jnp.sum(projected * projected, axis=-1, keepdims=True) + 1e-06)
    direction = projected * rinv
    cosine = jnp.sum(direction * target, axis=-1)
    grad_z = -loss_weight * rinv * (target - cosine[..., None] * direction)
    return (cosine, grad_z.astype(jnp.bfloat16))


def silu_slope(pre_act):
    sigma = jax.nn.sigmoid(pre_act)
    return sigma * (1.0 + pre_act * (1.0 - sigma))


def on_device(hidden, out_cot, proj_in, proj_out, attn_out_w, queries, keys, values, dino):
    features = lax.all_to_all(jnp.transpose(dino.reshape(48, 32, 128), (1, 0, 2)), "seq", split_axis=0, concat_axis=0, tiled=True).reshape(1, 1536, 128)
    target = unit_target(features)
    pre_act = jnp.einsum(
        "itd,dh->ith",
        lax.all_gather(hidden, "dp", axis=0, tiled=True),
        proj_in,
        preferred_element_type=jnp.float32,
    )
    silu_out = jax.nn.silu(pre_act).astype(jnp.bfloat16)
    picked = silu_out
    projected = lax.psum_scatter(
        jnp.einsum("ith,hc->itc", picked, proj_out, preferred_element_type=jnp.float32),
        "dp",
        scatter_dimension=0,
        tiled=True,
    )
    cosine, grad_z = cosine_grad(projected, target)
    grad_silu = jnp.einsum(
        "itc,hc->ith",
        lax.all_gather(grad_z, "dp", axis=0, tiled=True),
        proj_out,
        preferred_element_type=jnp.float32,
    )
    grad_pre = (grad_silu * silu_slope(pre_act)).astype(jnp.bfloat16)
    picked = grad_pre
    grad_repa = lax.psum_scatter(
        jnp.einsum("ith,dh->itd", picked, proj_in, preferred_element_type=jnp.float32),
        "dp",
        scatter_dimension=0,
        tiled=True,
    )
    grad_hidden = (out_cot.astype(jnp.float32) + grad_repa).astype(jnp.bfloat16)
    grad_attn = jnp.einsum(
        "itd,ed->ite", grad_hidden, attn_out_w, preferred_element_type=jnp.float32
    ).astype(jnp.bfloat16)
    def to_heads(x):
        blocks = x[0].T.reshape(NB, HD, x.shape[1])
        return lax.all_to_all(blocks, "seq", split_axis=0, concat_axis=0, tiled=True)

    def to_tokens(x):
        blocks = lax.all_to_all(x, "seq", split_axis=0, concat_axis=0, tiled=True)
        return blocks.reshape(NB * HD, x.shape[2]).T[None]

    grad_q, grad_k, grad_v = attention(to_heads(queries), to_heads(keys), to_heads(values), to_heads(grad_attn))
    back_q, back_k, back_v = to_tokens(grad_q), to_tokens(grad_k), to_tokens(grad_v)
    return (cosine, back_q, back_k, back_v)


def solution(mesh):
    in_specs = (
        P("dp", "seq", None),
        P("dp", "seq", None),
        P(None, "dp"),
        P("dp", None),
        P(),
        P("dp", "seq", None),
        P("dp", "seq", None),
        P("dp", "seq", None),
        P("dp", "seq", None),
    )
    out_specs = (P("dp", "seq"), P("dp", "seq", None), P("dp", "seq", None), P("dp", "seq", None))
    return jax.shard_map(
        on_device, mesh=mesh, in_specs=in_specs, out_specs=out_specs, check_vma=False
    )
```

```python
import jax
import jax.numpy as jnp
from jax import lax
from jax.experimental import pallas as pl
from jax.experimental.pallas import tpu as pltpu
from jax.sharding import PartitionSpec as P

LOG2E = 1.4426950408889634
F32=jnp.float32; BF=jnp.bfloat16
QB=512; KC=512; L=4096; NB=32; HD=64
T=128; D=2432; HID=1024; C=1536
MESH=pl.DeviceIdType.MESH
LOSS_WEIGHT=1000.0

def dot(a,b): return jnp.dot(a,b,preferred_element_type=F32)
def dot_nt(a,b): return lax.dot_general(a,b,(((1,),(1,)),((),())),preferred_element_type=F32)

def attn_kernel(x_ref,g_ref,o_ref, kk,vv,kt,vt, s_ref,u_ref, ak,av):
    i = pl.program_id(0)
    per = QB//128
    @pl.when(i==0)
    def _():
        for j in range(NB):
            kb=x_ref[j,HD:2*HD]; vb=x_ref[j,2*HD:]
            rows=pl.ds(j*128,128)
            kn=kb.T; vn=vb.T
            kk[rows,:]=jnp.concatenate([kn,kn],axis=1)
            lane=lax.broadcasted_iota(jnp.int32,(128,HD),1)
            vv[rows,:]=jnp.concatenate([vn,jnp.where(lane<2,1.0,0.0).astype(BF)],axis=1)
            kt[:,rows]=kb*BF(0.125)
            vt[pl.ds(0,HD),rows]=vb
        vt[pl.ds(HD,16),:]=jnp.ones((16,L),BF)
        ak[...]=jnp.zeros_like(ak); av[...]=jnp.zeros_like(av)
    qt=jnp.concatenate([x_ref[i*per+j,:HD] for j in range(per)],axis=1)
    gt=jnp.concatenate([g_ref[i*per+j] for j in range(per)],axis=1)
    qf=qt.astype(F32)*(0.125*LOG2E)
    qhi=qf.astype(BF); qlo=(qf-qhi.astype(F32)).astype(BF)
    qa=jnp.concatenate([qhi,qlo],axis=0)
    m=jnp.full((8,QB),-jnp.inf,F32)
    for c in range(L//KC):
        rows=pl.ds(c*KC,KC)
        s=dot(kk[rows,:],qa)
        s_ref[rows,:]=s
        m=jnp.maximum(m,jnp.max(s.reshape(KC//8,8,QB),axis=0))
    m=jnp.max(m,axis=0,keepdims=True)
    acc=jnp.zeros((HD+16,QB),F32)
    for c in range(L//KC):
        rows=pl.ds(c*KC,KC)
        u=jnp.exp2(s_ref[rows,:]-m).astype(BF)
        u_ref[rows,:]=u
        acc=acc+dot(vt[:,rows],u)
    l=acc[HD:HD+1]
    rl=1.0/l
    gf=gt.astype(F32)
    d=-jnp.sum(gf*acc[:HD],axis=0,keepdims=True)*rl
    dhi=d.astype(BF); dlo=(d-dhi.astype(F32))
    row=lax.broadcasted_iota(jnp.int32,(HD,QB),0)
    tail=jnp.where(row==0,dhi.astype(F32),jnp.where(row==1,dlo,0.0)).astype(BF)
    ga=jnp.concatenate([gt,tail],axis=0)
    qn=(qt.astype(F32)*(rl*0.125)).T.astype(BF)
    gn=(gf*rl).T.astype(BF)
    dq=jnp.zeros((HD,QB),F32)
    for c in range(L//KC):
        rows=pl.ds(c*KC,KC)
        u=u_ref[rows,:]
        dp=dot(vv[rows,:],ga)
        ds=(u.astype(F32)*dp).astype(BF)
        ak[rows,:]+=dot(ds,qn)
        av[rows,:]+=dot(u,gn)
        dq=dq+dot(kt[:,rows],ds)
    dq=(dq*rl).astype(BF)
    for j in range(per):
        o_ref[i*per+j,:HD]=dq[:,j*128:(j+1)*128]
    @pl.when(i==pl.num_programs(0)-1)
    def _():
        for j in range(NB):
            rows=pl.ds(j*128,128)
            o_ref[j,HD:2*HD]=ak[rows,:].T.astype(BF)
            o_ref[j,2*HD:]=av[rows,:].T.astype(BF)


def attention(x,g):
    xs=pl.BlockSpec((NB,3*HD,128),lambda i:(0,0,0))
    gs=pl.BlockSpec((NB,HD,128),lambda i:(0,0,0))
    return pl.pallas_call(attn_kernel,grid=(L//QB,),in_specs=[xs,gs],out_specs=xs,
        out_shape=jax.ShapeDtypeStruct((NB,3*HD,128),BF),
        scratch_shapes=[pltpu.VMEM((L,128),BF),pltpu.VMEM((L,128),BF),pltpu.VMEM((HD,L),BF),pltpu.VMEM((HD+16,L),BF),
            pltpu.VMEM((L,QB),F32),pltpu.VMEM((L,QB),BF),pltpu.VMEM((L,HD),F32),pltpu.VMEM((L,HD),F32)],
        compiler_params=pltpu.CompilerParams(vmem_limit_bytes=56*2**20),name="attention")(x,g)


def remote(src,dst,send,recv,dev):
    return pltpu.make_async_remote_copy(src_ref=src,dst_ref=dst,send_sem=send,recv_sem=recv,device_id=dev,device_id_type=MESH)


def wait_bytes(ref,sem):
    pltpu.make_async_copy(ref,ref,sem).wait()


def greet(devs_seq,dp,seq,extra):
    barrier=pltpu.get_barrier_semaphore()
    def hello(r,c):
        pl.semaphore_signal(barrier,inc=1,device_id=(dp,lax.rem(seq+r,NB)),device_id_type=MESH)
        return c
    lax.fori_loop(1,NB,hello,0)
    for dev in extra:
        pl.semaphore_signal(barrier,inc=1,device_id=dev,device_id_type=MESH)
    pl.semaphore_wait(barrier,NB-1+len(extra))


def front_kernel(hid,cot,q,k,v,wi_h,wo_h,wa_h,dino, cos_o,x_o,g_o,
        wi,wo,wa,xt,gt,feat,X,Z,pre,sil,p1s,p1c,p1p,p1r,p1q,p2s,p2c,p2p,p2r,p2q,
        wsem,xsem,fsem,gsem,hs,hr,zs,zr,s1,r1,s2,r2):
    dp=lax.axis_index("dp"); seq=lax.axis_index("seq")
    core=lax.rem(dp,2); hi=dp//2
    partner=(hi*2+(1-core),seq)
    cross_seq=lax.rem(seq+NB//2,NB)
    cross=((1-hi)*2+core,cross_seq)
    diag=((1-hi)*2+(1-core),cross_seq)
    loads=[pltpu.make_async_copy(a,b,wsem.at[n]) for n,(a,b) in enumerate(((wi_h,wi),(wo_h,wo),(wa_h,wa)))]
    for ld in loads: ld.start()
    greet(None,dp,seq,(partner,cross))
    H=T//2
    def half(ref,h): return ref.at[pl.ds(h*H,H)]
    hc=[remote(half(hid,h),X.at[2,pl.ds(h*H,H)],hs.at[h],hr.at[h],cross) for h in range(2)]
    hp=remote(hid,X.at[1],hs.at[2],hr.at[2],partner)
    hf=[remote(X.at[2,pl.ds(h*H,H)],X.at[3,pl.ds(h*H,H)],hs.at[3+h],hr.at[3+h],partner) for h in range(2)]
    for c in hc: c.start()
    hp.start()
    def send_feat(r,c):
        peer=lax.rem(seq+r,NB)
        remote(dino.at[:,pl.ds(pl.multiple_of(peer*T,T),T)],feat.at[seq],fsem.at[0],fsem.at[1],(dp,peer)).start()
        return c
    pltpu.make_async_copy(dino.at[:,pl.ds(pl.multiple_of(seq*T,T),T)],feat.at[seq],fsem.at[1]).start()
    def turn(p):
        cols=pl.ds(pl.multiple_of(p*T,T),T)
        for n,ref in enumerate((q,k,v)):
            t=ref[:,cols].T
            xt[2*p,pl.ds(n*HD,HD)]=t[:HD]
            xt[2*p+1,pl.ds(n*HD,HD)]=t[HD:]
    base=seq//2
    turn(base)
    pltpu.make_async_copy(xt.at[seq],x_o.at[seq],xsem.at[1]).start()
    mate=base*2+(1-lax.rem(seq,2))
    remote(xt.at[mate],x_o.at[seq],xsem.at[0],xsem.at[1],(dp,mate)).start()
    def turn_send(i,c):
        p=lax.rem(base+i,NB//2)
        turn(p)
        for e in range(2):
            remote(xt.at[2*p+e],x_o.at[seq],xsem.at[0],xsem.at[1],(dp,2*p+e)).start()
        return c
    lax.fori_loop(1,NB//2,turn_send,0)
    lax.fori_loop(1,NB,send_feat,0)
    X[0]=hid[...]
    loads[0].wait()
    hp.wait_recv()
    def first(at,rows):
        def body(n,c):
            cols=pl.ds(pl.multiple_of(n*256,256),256)
            y=dot(X[at:at+2].reshape(2*T,D),wi[:,cols])
            pre[pl.ds(rows,2*T),cols]=y
            sil[pl.ds(rows,2*T),cols]=(y/(1.0+jnp.exp(-y))).astype(BF)
            return c
        lax.fori_loop(0,HID//256,body,0)
    first(0,0)
    for h in range(2):
        hc[h].wait_recv(); hf[h].start()
    for h in range(2): hf[h].wait_recv()
    first(2,2*T)
    loads[1].wait()
    def second(n,c):
        cols=pl.ds(pl.multiple_of(n*256,256),256)
        y=dot(sil[2*T:],wo[:,cols])
        p1c[:,cols]=y[:T]
        p1s[0,:,cols]=y[T:].astype(BF)
        return c
    lax.fori_loop(0,C//256,second,0)
    c1=remote(p1s.at[0],p1r.at[0],s1.at[0],r1.at[0],partner); c1.start()
    def second_own(n,c):
        cols=pl.ds(pl.multiple_of(n*256,256),256)
        y=dot(sil[:2*T],wo[:,cols])
        p1q[:,cols]=y[:T]
        p1s[1,:,cols]=y[T:].astype(BF)
        return c
    lax.fori_loop(0,C//256,second_own,0)
    c2=remote(p1s.at[1],p1r.at[1],s1.at[1],r1.at[1],partner); c2.start()
    c1.wait_recv()
    p1p[...]=(p1c[...]+p1r[0].astype(F32)).astype(BF)
    c3=remote(p1p,p1r.at[2],s1.at[2],r1.at[2],cross); c3.start()
    wait_bytes(feat,fsem.at[1])
    f=feat[...].astype(F32)
    mean=jnp.sum(jnp.sum(f,axis=0),axis=0,keepdims=True)*(1.0/C)
    sh=f-mean[None]
    var=jnp.sum(jnp.sum(sh*sh,axis=0),axis=0,keepdims=True)*(1.0/C)
    sh=sh*lax.rsqrt(var+1e-6)[None]
    nn=jnp.sum(jnp.sum(sh*sh,axis=0),axis=0,keepdims=True)
    sh=sh*lax.rsqrt(nn+1e-6)[None]
    target=sh.reshape(C,T).T
    c2.wait_recv(); c3.wait_recv()
    pr=p1q[...]+p1r[1].astype(F32)+p1r[2].astype(F32)
    rinv=lax.rsqrt(jnp.sum(pr*pr,axis=1,keepdims=True)+1e-6)
    direction=pr*rinv
    cosine=jnp.sum(direction*target,axis=1,keepdims=True)
    ii=lax.broadcasted_iota(jnp.int32,(T,T),0); jj=lax.broadcasted_iota(jnp.int32,(T,T),1)
    cos_o[...]=jnp.sum(jnp.where(ii==jj,cosine,0.0),axis=0,keepdims=True)
    Z[0]=(-LOSS_WEIGHT*rinv*(target-cosine*direction)).astype(BF)
    zc=[remote(Z.at[0,pl.ds(h*H,H)],Z.at[2,pl.ds(h*H,H)],zs.at[h],zr.at[h],cross) for h in range(2)]
    zp=remote(Z.at[0],Z.at[1],zs.at[2],zr.at[2],partner)
    zf=[remote(Z.at[2,pl.ds(h*H,H)],Z.at[3,pl.ds(h*H,H)],zs.at[3+h],zr.at[3+h],partner) for h in range(2)]
    for c in zc: c.start()
    zp.start()
    zp.wait_recv()
    def back(at,rows):
        def body(n,c):
            cols=pl.ds(pl.multiple_of(n*256,256),256)
            gs=dot_nt(Z[at:at+2].reshape(2*T,C),wo[cols,:])
            y=pre[pl.ds(rows,2*T),cols]
            s=1.0/(1.0+jnp.exp(-y))
            sil[pl.ds(rows,2*T),cols]=(gs*(s*(1.0+y*(1.0-s)))).astype(BF)
            return c
        lax.fori_loop(0,HID//256,body,0)
    back(0,0)
    for h in range(2):
        zc[h].wait_recv(); zf[h].start()
    for h in range(2): zf[h].wait_recv()
    back(2,2*T)
    def third(n,c):
        cols=pl.ds(pl.multiple_of(n*128,128),128)
        y=dot_nt(sil[2*T:],wi[cols,:])
        p2c[:,cols]=y[:T]
        p2s[0,:,cols]=y[T:].astype(BF)
        return c
    lax.fori_loop(0,D//128,third,0)
    d1=remote(p2s.at[0],p2r.at[0],s2.at[0],r2.at[0],partner); d1.start()
    def third_own(n,c):
        cols=pl.ds(pl.multiple_of(n*128,128),128)
        y=dot_nt(sil[:2*T],wi[cols,:])
        p2q[:,cols]=y[:T]
        p2s[1,:,cols]=y[T:].astype(BF)
        return c
    d1.wait_recv()
    p2p[...]=(p2c[...]+p2r[0].astype(F32)).astype(BF)
    d3=remote(p2p,p2r.at[2],s2.at[2],r2.at[2],cross); d3.start()
    lax.fori_loop(0,D//128,third_own,0)
    d2=remote(p2s.at[1],p2r.at[1],s2.at[1],r2.at[1],partner); d2.start()
    loads[2].wait()
    d2.wait_recv(); d3.wait_recv()
    gh=(cot[...].astype(F32)+(p2q[...]+p2r[1].astype(F32)+p2r[2].astype(F32))).astype(BF)
    R=512
    def heads(i,c):
        at=lax.rem(seq//8+i,L//2//R)
        y=dot_nt(wa[pl.ds(pl.multiple_of(at*R,R),R)],Z2[...]).astype(BF)
        gt[pl.ds(at*8,8)]=y.reshape(8,HD,T)
        for e in range(8):
            h=at*8+lax.rem(seq+e,8)
            @pl.when(h!=seq)
            def _():
                remote(gt.at[h],g_o.at[seq],gsem.at[0],gsem.at[1],(dp,h)).start()
            @pl.when(h==seq)
            def _():
                pltpu.make_async_copy(gt.at[h],g_o.at[seq],gsem.at[1]).start()
        return c
    Z2=X.at[0]
    X[0]=gh
    lax.fori_loop(0,4,heads,0)
    for c in hc+[hp]+hf+zc+[zp]+zf+[c1,c2,c3,d1,d2,d3]: c.wait_send()
    wait_bytes(x_o,xsem.at[1]); wait_bytes(xt.at[pl.ds(0,NB-1)],xsem.at[0])
    wait_bytes(feat.at[pl.ds(0,NB-1)],fsem.at[0])
    wait_bytes(g_o,gsem.at[1]); wait_bytes(gt.at[pl.ds(0,NB-1)],gsem.at[0])


def front(hid,cot,q,k,v,wi,wo,wa,dino):
    vm=pl.BlockSpec(memory_space=pltpu.VMEM); hb=pl.BlockSpec(memory_space=pl.ANY)
    V=pltpu.VMEM; S=pltpu.SemaphoreType.DMA
    return pl.pallas_call(front_kernel,
        in_specs=[vm]*5+[hb]*3+[vm],out_specs=[vm,hb,hb],
        out_shape=[jax.ShapeDtypeStruct((1,T),F32),jax.ShapeDtypeStruct((NB,3*HD,T),BF),jax.ShapeDtypeStruct((NB,HD,T),BF)],
        scratch_shapes=[V((D,HID),BF),V((HID,C),BF),V((2048,D),BF),V((NB,3*HD,T),BF),V((NB,HD,T),BF),V((NB,48,T),BF),
            V((4,T,D),BF),V((4,T,C),BF),V((4*T,HID),F32),V((4*T,HID),BF),
            V((2,T,C),BF),V((T,C),F32),V((T,C),BF),V((3,T,C),BF),V((T,C),F32),
            V((2,T,D),BF),V((T,D),F32),V((T,D),BF),V((3,T,D),BF),V((T,D),F32),
            S((3,)),S((2,)),S((2,)),S((2,)),S((5,)),S((5,)),S((5,)),S((5,)),S((3,)),S((3,)),S((3,)),S((3,))],
        compiler_params=pltpu.CompilerParams(collective_id=0,has_side_effects=True,vmem_limit_bytes=56*2**20),
        name="front")(hid,cot,q,k,v,wi,wo,wa,dino)


def back_kernel(o_ref,q_o,k_o,v_o,buf,sem):
    dp=lax.axis_index("dp"); seq=lax.axis_index("seq")
    greet(None,dp,seq,())
    pltpu.make_async_copy(o_ref.at[seq],buf.at[seq],sem.at[1]).start()
    def send(r,c):
        peer=lax.rem(seq+r,NB)
        remote(o_ref.at[peer],buf.at[seq],sem.at[0],sem.at[1],(dp,peer)).start()
        return c
    lax.fori_loop(1,NB,send,0)
    wait_bytes(buf,sem.at[1])
    for n,ref in enumerate((q_o,k_o,v_o)):
        for p in range(NB//2):
            ref[:,p*T:(p+1)*T]=buf[2*p:2*p+2,n*HD:(n+1)*HD].reshape(T,T).T
    wait_bytes(buf.at[pl.ds(0,NB-1)],sem.at[0])


def back(o):
    vm=pl.BlockSpec(memory_space=pltpu.VMEM)
    return pl.pallas_call(back_kernel,in_specs=[vm],out_specs=[vm]*3,
        out_shape=[jax.ShapeDtypeStruct((T,NB*HD),BF)]*3,
        scratch_shapes=[pltpu.VMEM((NB,3*HD,T),BF),pltpu.SemaphoreType.DMA((2,))],
        compiler_params=pltpu.CompilerParams(collective_id=1,has_side_effects=True,vmem_limit_bytes=32*2**20),
        name="back")(o)


def on_device(hidden,out_cot,proj_in,proj_out,attn_out_w,queries,keys,values,dino):
    cosine,x,g=front(hidden[0],out_cot[0],queries[0],keys[0],values[0],proj_in,proj_out,attn_out_w,dino[0])
    gq,gk,gv=back(attention(x,g))
    return cosine,gq[None],gk[None],gv[None]


def solution(mesh):
    in_specs = (
        P("dp", "seq", None),
        P("dp", "seq", None),
        P(None, "dp"),
        P("dp", None),
        P(),
        P("dp", "seq", None),
        P("dp", "seq", None),
        P("dp", "seq", None),
        P("dp", "seq", None),
    )
    out_specs = (P("dp", "seq"), P("dp", "seq", None), P("dp", "seq", None), P("dp", "seq", None))
    return jax.shard_map(
        on_device, mesh=mesh, in_specs=in_specs, out_specs=out_specs, check_vma=False
    )
```

```python
import jax
import jax.numpy as jnp
from jax import lax
from jax.experimental import pallas as pl
from jax.experimental.pallas import tpu as pltpu
from jax.sharding import PartitionSpec as P

LOG2E = 1.4426950408889634
F32=jnp.float32; BF=jnp.bfloat16
QB=256; KC=256; QP=512; KB=512; L=4096; NB=32; HD=64
T=128; D=2432; HID=1024; C=1536
NQ=L//QB
MESH=pl.DeviceIdType.MESH
LOSS_WEIGHT=1000.0

def dot(a,b): return jnp.dot(a,b,preferred_element_type=F32)
def dot_nt(a,b): return lax.dot_general(a,b,(((1,),(1,)),((),())),preferred_element_type=F32)

def scores_prep(x,kk,vt):
    for j in range(NB):
        rows=pl.ds(j*T,T)
        kn=x[j,HD:2*HD].T
        kk[rows,:]=jnp.concatenate([kn,kn],axis=1)
        vt[pl.ds(0,HD),rows]=x[j,2*HD:]
    vt[pl.ds(HD,16),:]=jnp.ones((16,L),BF)


def stage(i,x,kk,vt,sn,so,m,u_ref,a_ref,first=False,last=False):
    per=QB//T
    if not last:
        qt=jnp.concatenate([x[i*per+j,:HD] for j in range(per)],axis=1)
        qf=qt.astype(F32)*(0.125*LOG2E)
        qhi=qf.astype(BF); qlo=(qf-qhi.astype(F32)).astype(BF)
        qa=jnp.concatenate([qhi,qlo],axis=0)
    mn=jnp.full((8,QB),-jnp.inf,F32)
    acc=jnp.zeros((HD+16,QB),F32)
    for c in range(L//KC):
        rows=pl.ds(c*KC,KC)
        if not last:
            y=dot(kk[rows,:],qa)
            sn[rows,:]=y
            mn=jnp.maximum(mn,jnp.max(y.reshape(KC//8,8,QB),axis=0))
        if not first:
            u=jnp.exp2(so[rows,:]-m).astype(BF)
            u_ref[rows,:]=u
            acc=acc+dot(vt[:,rows],u)
    if not first:
        j=i-1
        a_ref[:,pl.ds(j*QB if isinstance(j,int) else pl.multiple_of(j*QB,QB),QB)]=acc
    return jnp.max(mn,axis=0,keepdims=True)


def grads_prep(x,g_ref,a_ref,vv,kt,ga,qn,gn,rlr):
    lane=lax.broadcasted_iota(jnp.int32,(T,HD),1)
    ones=jnp.where(lane<2,1.0,0.0).astype(BF)
    row=lax.broadcasted_iota(jnp.int32,(HD,T),0)
    for j in range(NB):
        rows=pl.ds(j*T,T)
        vv[rows,:]=jnp.concatenate([x[j,2*HD:].T,ones],axis=1)
        kt[:,rows]=x[j,HD:2*HD]*BF(0.125)
        a=a_ref[:,rows]
        rl=1.0/a[HD:HD+1]
        rlr[0:1,rows]=rl
        gt=g_ref[j]; gf=gt.astype(F32)
        d=-jnp.sum(gf*a[:HD],axis=0,keepdims=True)*rl
        dhi=d.astype(BF); dlo=d-dhi.astype(F32)
        ga[pl.ds(0,HD),rows]=gt
        ga[pl.ds(HD,HD),rows]=jnp.where(row==0,dhi.astype(F32),jnp.where(row==1,dlo,0.0)).astype(BF)
        qn[rows,:]=(x[j,:HD].astype(F32)*(rl*0.125)).T.astype(BF)
        gn[rows,:]=(gf*rl).T.astype(BF)


def remote(src,dst,send,recv,dev):
    return pltpu.make_async_remote_copy(src_ref=src,dst_ref=dst,send_sem=send,recv_sem=recv,device_id=dev,device_id_type=MESH)


def wait_bytes(ref,sem):
    pltpu.make_async_copy(ref,ref,sem).wait()


def greet(dp,seq,extra):
    barrier=pltpu.get_barrier_semaphore()
    def hello(r,c):
        pl.semaphore_signal(barrier,inc=1,device_id=(dp,lax.rem(seq+r,NB)),device_id_type=MESH)
        return c
    lax.fori_loop(1,NB,hello,0)
    for dev in extra:
        pl.semaphore_signal(barrier,inc=1,device_id=dev,device_id_type=MESH)


def meet(extra):
    pl.semaphore_wait(pltpu.get_barrier_semaphore(),NB-1+extra)


def front_kernel(hid,cot,q,k,v,wi_h,wo_h,wa_h,dino, cos_o,x_o,g_o,u_o,a_o,
        wi,wo,wa,xt,gt,feat,X,Z,pre,sil,p1s,p1c,p1p,p1r,p1q,p2s,p2c,p2p,p2r,p2q,
        xh,kk,vt,sa,sb,ua,ub,wsem,xsem,fsem,gsem,hs,hr,zs,zr,s1,r1,s2,r2,usem,osem):
    dp=lax.axis_index("dp"); seq=lax.axis_index("seq")
    core=lax.rem(dp,2); hi=dp//2
    partner=(hi*2+(1-core),seq)
    cross_seq=lax.rem(seq+NB//2,NB)
    cross=((1-hi)*2+core,cross_seq)
    diag=((1-hi)*2+(1-core),cross_seq)
    loads=[pltpu.make_async_copy(a,b,wsem.at[n]) for n,(a,b) in enumerate(((wi_h,wi),(wo_h,wo),(wa_h,wa)))]
    for ld in loads: ld.start()
    greet(dp,seq,(partner,cross))
    meet(2)
    H=T//2
    def half(ref,h): return ref.at[pl.ds(h*H,H)]
    def ucopy(i,n): return pltpu.make_async_copy((ua,ub)[n],u_o.at[i],usem.at[n])
    def pairs(lo,hi_,m):
        def body(p,m):
            i=2*p+1
            @pl.when(p>0)
            def _(): ucopy(0,0).wait()
            m=stage(i,xh,kk,vt,sb,sa,m,ua,a_o)
            ucopy(i-1,0).start()
            @pl.when(p>0)
            def _(): ucopy(0,1).wait()
            m=stage(i+1,xh,kk,vt,sa,sb,m,ub,a_o)
            ucopy(i,1).start()
            return m
        return lax.fori_loop(lo,hi_,body,m)
    hc=[remote(half(hid,h),X.at[2,pl.ds(h*H,H)],hs.at[h],hr.at[h],cross) for h in range(2)]
    hp=remote(hid,X.at[1],hs.at[2],hr.at[2],partner)
    hf=[remote(X.at[2,pl.ds(h*H,H)],X.at[3,pl.ds(h*H,H)],hs.at[3+h],hr.at[3+h],partner) for h in range(2)]
    for c in hc: c.start()
    hp.start()
    def send_feat(r,c):
        peer=lax.rem(seq+r,NB)
        remote(dino.at[:,pl.ds(pl.multiple_of(peer*T,T),T)],feat.at[seq],fsem.at[0],fsem.at[1],(dp,peer)).start()
        return c
    pltpu.make_async_copy(dino.at[:,pl.ds(pl.multiple_of(seq*T,T),T)],feat.at[seq],fsem.at[1]).start()
    def turn(p):
        cols=pl.ds(pl.multiple_of(p*T,T),T)
        for n,ref in enumerate((q,k,v)):
            t=ref[:,cols].T
            xt[2*p,pl.ds(n*HD,HD)]=t[:HD]
            xt[2*p+1,pl.ds(n*HD,HD)]=t[HD:]
    base=seq//2
    turn(base)
    pltpu.make_async_copy(xt.at[seq],xh.at[seq],xsem.at[1]).start()
    mate=base*2+(1-lax.rem(seq,2))
    remote(xt.at[mate],xh.at[seq],xsem.at[0],xsem.at[1],(dp,mate)).start()
    def turn_send(i,c):
        p=lax.rem(base+i,NB//2)
        turn(p)
        for e in range(2):
            remote(xt.at[2*p+e],xh.at[seq],xsem.at[0],xsem.at[1],(dp,2*p+e)).start()
        return c
    lax.fori_loop(1,NB//2,turn_send,0)
    lax.fori_loop(1,NB,send_feat,0)
    X[0]=hid[...]
    loads[0].wait()
    hp.wait_recv()
    def first(at,rows):
        def body(n,c):
            cols=pl.ds(pl.multiple_of(n*256,256),256)
            y=dot(X[at:at+2].reshape(2*T,D),wi[:,cols])
            pre[pl.ds(rows,2*T),cols]=y
            sil[pl.ds(rows,2*T),cols]=(y/(1.0+jnp.exp(-y))).astype(BF)
            return c
        lax.fori_loop(0,HID//256,body,0)
    first(0,0)
    for h in range(2):
        hc[h].wait_recv(); hf[h].start()
    for h in range(2): hf[h].wait_recv()
    first(2,2*T)
    loads[1].wait()
    def second(n,c):
        cols=pl.ds(pl.multiple_of(n*256,256),256)
        y=dot(sil[2*T:],wo[:,cols])
        p1c[:,cols]=y[:T]
        p1s[0,:,cols]=y[T:].astype(BF)
        return c
    lax.fori_loop(0,C//256,second,0)
    c1=remote(p1s.at[0],p1r.at[0],s1.at[0],r1.at[0],partner); c1.start()
    def second_own(n,c):
        cols=pl.ds(pl.multiple_of(n*256,256),256)
        y=dot(sil[:2*T],wo[:,cols])
        p1q[:,cols]=y[:T]
        p1s[1,:,cols]=y[T:].astype(BF)
        return c
    lax.fori_loop(0,C//256,second_own,0)
    c2=remote(p1s.at[1],p1r.at[1],s1.at[1],r1.at[1],partner); c2.start()
    c1.wait_recv()
    p1p[...]=(p1c[...]+p1r[0].astype(F32)).astype(BF)
    c3=remote(p1p,p1r.at[2],s1.at[2],r1.at[2],cross); c3.start()
    wait_bytes(feat,fsem.at[1])
    f=feat[...].astype(F32)
    mean=jnp.sum(jnp.sum(f,axis=0),axis=0,keepdims=True)*(1.0/C)
    sh=f-mean[None]
    var=jnp.sum(jnp.sum(sh*sh,axis=0),axis=0,keepdims=True)*(1.0/C)
    sh=sh*lax.rsqrt(var+1e-6)[None]
    nn=jnp.sum(jnp.sum(sh*sh,axis=0),axis=0,keepdims=True)
    sh=sh*lax.rsqrt(nn+1e-6)[None]
    target=sh.reshape(C,T).T
    wait_bytes(xh,xsem.at[1])
    xcopy=pltpu.make_async_copy(xh,x_o,osem); xcopy.start()
    scores_prep(xh,kk,vt)
    m=stage(0,xh,kk,vt,sa,None,None,None,None,first=True)
    m=pairs(0,2,m)
    c2.wait_recv(); c3.wait_recv()
    pr=p1q[...]+p1r[1].astype(F32)+p1r[2].astype(F32)
    rinv=lax.rsqrt(jnp.sum(pr*pr,axis=1,keepdims=True)+1e-6)
    direction=pr*rinv
    cosine=jnp.sum(direction*target,axis=1,keepdims=True)
    ii=lax.broadcasted_iota(jnp.int32,(T,T),0); jj=lax.broadcasted_iota(jnp.int32,(T,T),1)
    cos_o[...]=jnp.sum(jnp.where(ii==jj,cosine,0.0),axis=0,keepdims=True)
    Z[0]=(-LOSS_WEIGHT*rinv*(target-cosine*direction)).astype(BF)
    zc=[remote(Z.at[0,pl.ds(h*H,H)],Z.at[2,pl.ds(h*H,H)],zs.at[h],zr.at[h],cross) for h in range(2)]
    zp=remote(Z.at[0],Z.at[1],zs.at[2],zr.at[2],partner)
    zf=[remote(Z.at[2,pl.ds(h*H,H)],Z.at[3,pl.ds(h*H,H)],zs.at[3+h],zr.at[3+h],partner) for h in range(2)]
    for c in zc: c.start()
    zp.start()
    zp.wait_recv()
    def back(at,rows):
        def body(n,c):
            cols=pl.ds(pl.multiple_of(n*256,256),256)
            gs=dot_nt(Z[at:at+2].reshape(2*T,C),wo[cols,:])
            y=pre[pl.ds(rows,2*T),cols]
            s=1.0/(1.0+jnp.exp(-y))
            sil[pl.ds(rows,2*T),cols]=(gs*(s*(1.0+y*(1.0-s)))).astype(BF)
            return c
        lax.fori_loop(0,HID//256,body,0)
    back(0,0)
    m=pairs(2,3,m)
    for h in range(2):
        zc[h].wait_recv(); zf[h].start()
        m=pairs(3+h,4+h,m)
    for h in range(2): zf[h].wait_recv()
    back(2,2*T)
    def third(n,c):
        cols=pl.ds(pl.multiple_of(n*128,128),128)
        y=dot_nt(sil[2*T:],wi[cols,:])
        p2c[:,cols]=y[:T]
        p2s[0,:,cols]=y[T:].astype(BF)
        return c
    lax.fori_loop(0,D//128,third,0)
    d1=remote(p2s.at[0],p2r.at[0],s2.at[0],r2.at[0],partner); d1.start()
    def third_own(n,c):
        cols=pl.ds(pl.multiple_of(n*128,128),128)
        y=dot_nt(sil[:2*T],wi[cols,:])
        p2q[:,cols]=y[:T]
        p2s[1,:,cols]=y[T:].astype(BF)
        return c
    d1.wait_recv()
    p2p[...]=(p2c[...]+p2r[0].astype(F32)).astype(BF)
    d3=remote(p2p,p2r.at[2],s2.at[2],r2.at[2],cross); d3.start()
    lax.fori_loop(0,D//128,third_own,0)
    d2=remote(p2s.at[1],p2r.at[1],s2.at[1],r2.at[1],partner); d2.start()
    m=pairs(5,7,m)
    ucopy(0,0).wait()
    m=stage(NQ-1,xh,kk,vt,sb,sa,m,ua,a_o)
    ucopy(NQ-2,0).start()
    ucopy(0,1).wait()
    stage(NQ,xh,kk,vt,None,sb,m,ub,a_o,last=True)
    ucopy(NQ-1,1).start()
    loads[2].wait()
    d2.wait_recv(); d3.wait_recv()
    gh=(cot[...].astype(F32)+(p2q[...]+p2r[1].astype(F32)+p2r[2].astype(F32))).astype(BF)
    R=512
    def heads(i,c):
        at=lax.rem(seq//8+i,L//2//R)
        y=dot_nt(wa[pl.ds(pl.multiple_of(at*R,R),R)],Z2[...]).astype(BF)
        gt[pl.ds(at*8,8)]=y.reshape(8,HD,T)
        for e in range(8):
            h=at*8+lax.rem(seq+e,8)
            @pl.when(h!=seq)
            def _():
                remote(gt.at[h],g_o.at[seq],gsem.at[0],gsem.at[1],(dp,h)).start()
            @pl.when(h==seq)
            def _():
                pltpu.make_async_copy(gt.at[h],g_o.at[seq],gsem.at[1]).start()
        return c
    Z2=X.at[0]
    X[0]=gh
    lax.fori_loop(0,4,heads,0)
    xcopy.wait()
    for n in range(2): ucopy(n,n).wait()
    for c in hc+[hp]+hf+zc+[zp]+zf+[c1,c2,c3,d1,d2,d3]: c.wait_send()
    wait_bytes(xt.at[pl.ds(0,NB-1)],xsem.at[0])
    wait_bytes(feat.at[pl.ds(0,NB-1)],fsem.at[0])
    wait_bytes(g_o,gsem.at[1]); wait_bytes(gt.at[pl.ds(0,NB-1)],gsem.at[0])


def front(hid,cot,q,k,v,wi,wo,wa,dino):
    vm=pl.BlockSpec(memory_space=pltpu.VMEM); hb=pl.BlockSpec(memory_space=pl.ANY)
    V=pltpu.VMEM; S=pltpu.SemaphoreType.DMA
    return pl.pallas_call(front_kernel,
        in_specs=[vm]*5+[hb]*3+[vm],out_specs=[vm,hb,hb,hb,vm],
        out_shape=[jax.ShapeDtypeStruct((1,T),F32),jax.ShapeDtypeStruct((NB,3*HD,T),BF),jax.ShapeDtypeStruct((NB,HD,T),BF),
            jax.ShapeDtypeStruct((NQ,L,QB),BF),jax.ShapeDtypeStruct((HD+16,L),F32)],
        scratch_shapes=[V((D,HID),BF),V((HID,C),BF),V((2048,D),BF),V((NB,3*HD,T),BF),V((NB,HD,T),BF),V((NB,48,T),BF),
            V((4,T,D),BF),V((4,T,C),BF),V((4*T,HID),F32),V((4*T,HID),BF),
            V((2,T,C),BF),V((T,C),F32),V((T,C),BF),V((3,T,C),BF),V((T,C),F32),
            V((2,T,D),BF),V((T,D),F32),V((T,D),BF),V((3,T,D),BF),V((T,D),F32),
            V((NB,3*HD,T),BF),V((L,T),BF),V((HD+16,L),BF),V((L,QB),F32),V((L,QB),F32),V((L,QB),BF),V((L,QB),BF),
            S((3,)),S((2,)),S((2,)),S((2,)),S((5,)),S((5,)),S((5,)),S((5,)),S((3,)),S((3,)),S((3,)),S((3,)),S((2,)),S],
        compiler_params=pltpu.CompilerParams(collective_id=0,has_side_effects=True,vmem_limit_bytes=62*2**20),
        name="front")(hid,cot,q,k,v,wi,wo,wa,dino)


def finish_kernel(x_ref,g_ref,a_ref,u_h,q_o,k_o,v_o,vv,kt,ga,qn,gn,rlr,dq,u_ref,o_ref,buf,usem,ksem,qsem):
    dp=lax.axis_index("dp"); seq=lax.axis_index("seq")
    NK=L//KB; per=KB//T
    first=seq//per
    def place(b): return lax.rem(b+first,NK)
    def fetch(b):
        slot=lax.rem(b,2)
        return pltpu.make_async_copy(u_h.at[:,pl.ds(pl.multiple_of(place(b)*KB,KB),KB)],u_ref.at[slot],usem.at[slot])
    fetch(0).start()
    greet(dp,seq,())
    grads_prep(x_ref,g_ref,a_ref,vv,kt,ga,qn,gn,rlr)
    dq[...]=jnp.zeros_like(dq)
    meet(0)
    def give(h,part,sem):
        @pl.when(h!=seq)
        def _():
            remote(o_ref.at[h,part],buf.at[seq,part],sem.at[0],sem.at[1],(dp,h)).start()
        @pl.when(h==seq)
        def _():
            pltpu.make_async_copy(o_ref.at[h,part],buf.at[seq,part],sem.at[1]).start()
    def body(b,c):
        slot=lax.rem(b,2)
        @pl.when(b<NK-1)
        def _(): fetch(b+1).start()
        fetch(b).wait()
        at=place(b)
        kr=pl.ds(pl.multiple_of(at*KB,KB),KB)
        v=vv[kr,:]; k=kt[:,kr]
        dk=jnp.zeros((KB,HD),F32); dv=jnp.zeros((KB,HD),F32)
        for i in range(L//QP):
            qr=pl.ds(i*QP,QP)
            n=QP//QB
            u=jnp.concatenate([u_ref[slot,i*n+e] for e in range(n)],axis=1)
            ds=(u.astype(F32)*dot(v,ga[:,qr])).astype(BF)
            dk=dk+dot(ds,qn[qr,:]); dv=dv+dot(u,gn[qr,:])
            dq[:,qr]+=dot(k,ds)
        for j in range(per):
            o_ref[at*per+j,HD:2*HD]=dk[j*T:(j+1)*T].T.astype(BF)
            o_ref[at*per+j,2*HD:]=dv[j*T:(j+1)*T].T.astype(BF)
        for j in range(per):
            give(at*per+lax.rem(seq+j,per),pl.ds(HD,2*HD),ksem)
        return c
    lax.fori_loop(0,NK,body,0)
    for j in range(NB):
        o_ref[j,:HD]=(dq[:,j*T:(j+1)*T]*rlr[0:1,j*T:(j+1)*T]).astype(BF)
    def send(r,c):
        give(lax.rem(seq+r,NB),pl.ds(0,HD),qsem)
        return c
    lax.fori_loop(0,NB,send,0)
    kpart=buf.at[:,pl.ds(HD,2*HD)]
    wait_bytes(kpart,ksem.at[1])
    def out(ref,n):
        for p in range(NB//2):
            ref[:,p*T:(p+1)*T]=buf[2*p:2*p+2,n*HD:(n+1)*HD].reshape(T,T).T
    out(k_o,1); out(v_o,2)
    qpart=buf.at[:,pl.ds(0,HD)]
    wait_bytes(qpart,qsem.at[1])
    out(q_o,0)
    wait_bytes(buf.at[pl.ds(0,NB-1),pl.ds(HD,2*HD)],ksem.at[0])
    wait_bytes(buf.at[pl.ds(0,NB-1),pl.ds(0,HD)],qsem.at[0])


def finish(x,g,u,a):
    V=pltpu.VMEM; S=pltpu.SemaphoreType.DMA
    vm=pl.BlockSpec(memory_space=V); hb=pl.BlockSpec(memory_space=pl.ANY)
    return pl.pallas_call(finish_kernel,in_specs=[vm]*3+[hb],out_specs=[vm]*3,
        out_shape=[jax.ShapeDtypeStruct((T,NB*HD),BF)]*3,
        scratch_shapes=[V((L,T),BF),V((HD,L),BF),V((T,L),BF),V((L,HD),BF),V((L,HD),BF),V((8,L),F32),V((HD,L),F32),
            V((2,NQ,KB,QB),BF),V((NB,3*HD,T),BF),V((NB,3*HD,T),BF),S((2,)),S((2,)),S((2,))],
        compiler_params=pltpu.CompilerParams(collective_id=1,has_side_effects=True,vmem_limit_bytes=56*2**20),
        name="finish")(x,g,a,u)


def on_device(hidden,out_cot,proj_in,proj_out,attn_out_w,queries,keys,values,dino):
    cosine,x,g,u,a=front(hidden[0],out_cot[0],queries[0],keys[0],values[0],proj_in,proj_out,attn_out_w,dino[0])
    gq,gk,gv=finish(x,g,u,a)
    return cosine,gq[None],gk[None],gv[None]


def solution(mesh):
    in_specs = (
        P("dp", "seq", None),
        P("dp", "seq", None),
        P(None, "dp"),
        P("dp", None),
        P(),
        P("dp", "seq", None),
        P("dp", "seq", None),
        P("dp", "seq", None),
        P("dp", "seq", None),
    )
    out_specs = (P("dp", "seq"), P("dp", "seq", None), P("dp", "seq", None), P("dp", "seq", None))
    return jax.shard_map(
        on_device, mesh=mesh, in_specs=in_specs, out_specs=out_specs, check_vma=False
    )
```

```python
import jax
import jax.numpy as jnp
from jax import lax
from jax.experimental import pallas as pl
from jax.experimental.pallas import tpu as pltpu
from jax.sharding import PartitionSpec as P

LOG2E = 1.4426950408889634
F32=jnp.float32; BF=jnp.bfloat16
QB=256; KC=256; QP=512; KB=512; L=4096; NB=32; HD=64
T=128; D=2432; HID=1024; C=1536
NQ=L//QB
MESH=pl.DeviceIdType.MESH
LOSS_WEIGHT=1000.0

def dot(a,b): return jnp.dot(a,b,preferred_element_type=F32)
def dot_nt(a,b): return lax.dot_general(a,b,(((1,),(1,)),((),())),preferred_element_type=F32)

def scores_prep(x,kk,vt):
    for j in range(NB):
        rows=pl.ds(j*T,T)
        kn=x[j,HD:2*HD].T
        kk[rows,:]=jnp.concatenate([kn,kn],axis=1)
        vt[pl.ds(0,HD),rows]=x[j,2*HD:]
    vt[pl.ds(HD,16),:]=jnp.ones((16,L),BF)


def stage(i,x,kk,vt,sn,so,m,u_ref,a_ref,first=False,last=False):
    per=QB//T
    if not last:
        qt=jnp.concatenate([x[i*per+j,:HD] for j in range(per)],axis=1)
        qf=qt.astype(F32)*(0.125*LOG2E)
        qhi=qf.astype(BF); qlo=(qf-qhi.astype(F32)).astype(BF)
        qa=jnp.concatenate([qhi,qlo],axis=0)
    mn=jnp.full((8,QB),-jnp.inf,F32)
    acc=jnp.zeros((HD+16,QB),F32)
    for c in range(L//KC):
        rows=pl.ds(c*KC,KC)
        if not last:
            y=dot(kk[rows,:],qa)
            sn[rows,:]=y
            mn=jnp.maximum(mn,jnp.max(y.reshape(KC//8,8,QB),axis=0))
        if not first:
            u=jnp.exp2(so[rows,:]-m).astype(BF)
            u_ref[rows,:]=u
            acc=acc+dot(vt[:,rows],u)
    if not first:
        j=i-1
        a_ref[:,pl.ds(j*QB if isinstance(j,int) else pl.multiple_of(j*QB,QB),QB)]=acc
    return jnp.max(mn,axis=0,keepdims=True)


def grads_prep(x,g_ref,a_ref,vv,kt,ga,qn,gn,rlr):
    lane=lax.broadcasted_iota(jnp.int32,(T,HD),1)
    ones=jnp.where(lane<2,1.0,0.0).astype(BF)
    row=lax.broadcasted_iota(jnp.int32,(HD,T),0)
    for j in range(NB):
        rows=pl.ds(j*T,T)
        vv[rows,:]=jnp.concatenate([x[j,2*HD:].T,ones],axis=1)
        kt[:,rows]=x[j,HD:2*HD]*BF(0.125)
        a=a_ref[:,rows]
        rl=1.0/a[HD:HD+1]
        rlr[0:1,rows]=rl
        gt=g_ref[j]; gf=gt.astype(F32)
        d=-jnp.sum(gf*a[:HD],axis=0,keepdims=True)*rl
        dhi=d.astype(BF); dlo=d-dhi.astype(F32)
        ga[pl.ds(0,HD),rows]=gt
        ga[pl.ds(HD,HD),rows]=jnp.where(row==0,dhi.astype(F32),jnp.where(row==1,dlo,0.0)).astype(BF)
        qn[rows,:]=(x[j,:HD].astype(F32)*(rl*0.125)).T.astype(BF)
        gn[rows,:]=(gf*rl).T.astype(BF)


def remote(src,dst,send,recv,dev):
    return pltpu.make_async_remote_copy(src_ref=src,dst_ref=dst,send_sem=send,recv_sem=recv,device_id=dev,device_id_type=MESH)


def wait_bytes(ref,sem):
    pltpu.make_async_copy(ref,ref,sem).wait()


def greet(dp,seq,extra):
    barrier=pltpu.get_barrier_semaphore()
    def hello(r,c):
        pl.semaphore_signal(barrier,inc=1,device_id=(dp,lax.rem(seq+r,NB)),device_id_type=MESH)
        return c
    lax.fori_loop(1,NB,hello,0)
    for dev in extra:
        pl.semaphore_signal(barrier,inc=1,device_id=dev,device_id_type=MESH)


def meet(extra):
    pl.semaphore_wait(pltpu.get_barrier_semaphore(),NB-1+extra)


def front_kernel(hid,cot,q,k,v,wi_h,wo_h,wa_h,dino, cos_o,x_o,g_o,u_o,a_o,
        wi,wo,wa,xt,gt,feat,X,Z,pre,sil,p1s,p1c,p1p,p1r,p1q,p2s,p2c,p2p,p2r,p2q,target,gh,
        xh,kk,vt,sa,sb,ua,ub,wsem,xsem,fsem,gsem,hs,hr,zs,zr,s1,r1,s2,r2,usem,osem):
    dp=lax.axis_index("dp"); seq=lax.axis_index("seq")
    core=lax.rem(dp,2); hi=dp//2
    partner=(hi*2+(1-core),seq)
    cross_seq=lax.rem(seq+NB//2,NB)
    cross=((1-hi)*2+core,cross_seq)
    diag=((1-hi)*2+(1-core),cross_seq)
    loads=[pltpu.make_async_copy(a,b,wsem.at[n]) for n,(a,b) in enumerate(((wi_h,wi),(wo_h,wo),(wa_h,wa)))]
    for ld in loads: ld.start()
    greet(dp,seq,(partner,cross))
    meet(2)
    H=T//2
    def ucopy(i,n): return pltpu.make_async_copy((ua,ub)[n],u_o.at[i],usem.at[n])
    def pairs(lo,hi_,m):
        def body(p,m):
            i=2*p+1
            @pl.when(p>0)
            def _(): ucopy(0,0).wait()
            m=stage(i,xh,kk,vt,sb,sa,m,ua,a_o)
            ucopy(i-1,0).start()
            @pl.when(p>0)
            def _(): ucopy(0,1).wait()
            m=stage(i+1,xh,kk,vt,sa,sb,m,ub,a_o)
            ucopy(i,1).start()
            return m
        return lax.fori_loop(lo,hi_,body,m)
    hc=[remote(hid.at[pl.ds(h*H,H)],X.at[h,2],hs.at[h],hr.at[h],cross) for h in range(2)]
    hp=[remote(hid.at[pl.ds(h*H,H)],X.at[h,1],hs.at[2+h],hr.at[2+h],partner) for h in range(2)]
    hf=[remote(X.at[h,2],X.at[h,3],hs.at[4+h],hr.at[4+h],partner) for h in range(2)]
    hc[0].start(); hp[0].start(); hc[1].start(); hp[1].start()
    def send_feat(r,c):
        peer=lax.rem(seq+r,NB)
        remote(dino.at[:,pl.ds(pl.multiple_of(peer*T,T),T)],feat.at[seq],fsem.at[0],fsem.at[1],(dp,peer)).start()
        return c
    pltpu.make_async_copy(dino.at[:,pl.ds(pl.multiple_of(seq*T,T),T)],feat.at[seq],fsem.at[1]).start()
    lax.fori_loop(1,NB,send_feat,0)
    def turn(p):
        cols=pl.ds(pl.multiple_of(p*T,T),T)
        for n,ref in enumerate((q,k,v)):
            t=ref[:,cols].T
            xt[2*p,pl.ds(n*HD,HD)]=t[:HD]
            xt[2*p+1,pl.ds(n*HD,HD)]=t[HD:]
    base=seq//2
    turn(base)
    pltpu.make_async_copy(xt.at[seq],xh.at[seq],xsem.at[1]).start()
    mate=base*2+(1-lax.rem(seq,2))
    remote(xt.at[mate],xh.at[seq],xsem.at[0],xsem.at[1],(dp,mate)).start()
    def turn_send(i,c):
        p=lax.rem(base+i,NB//2)
        turn(p)
        for e in range(2):
            remote(xt.at[2*p+e],xh.at[seq],xsem.at[0],xsem.at[1],(dp,2*p+e)).start()
        return c
    lax.fori_loop(1,NB//2,turn_send,0)
    def first(h):
        def body(n,c):
            cols=pl.ds(pl.multiple_of(n*256,256),256)
            y=dot(X[h].reshape(4*H,D),wi[:,cols])
            pre[h,:,cols]=y
            sil[h,:,cols]=(y/(1.0+jnp.exp(-y))).astype(BF)
            return c
        lax.fori_loop(0,HID//256,body,0)
    def second(h):
        def body(n,c):
            cols=pl.ds(pl.multiple_of(n*256,256),256)
            y=dot(sil[h],wo[:,cols])
            p1q[h,:,cols]=y[:H]
            p1s[h,1,:,cols]=y[H:2*H].astype(BF)
            p1c[h,:,cols]=y[2*H:3*H]
            p1s[h,0,:,cols]=y[3*H:].astype(BF)
            return c
        lax.fori_loop(0,C//256,body,0)
    def trio(sent,summed,recv,ss,rs):
        return [[remote(sent.at[h,0],recv.at[h,0],ss.at[h,0],rs.at[h,0],partner),
            remote(sent.at[h,1],recv.at[h,1],ss.at[h,1],rs.at[h,1],partner),
            remote(summed.at[h],recv.at[h,2],ss.at[h,2],rs.at[h,2],cross)] for h in range(2)]
    cs=trio(p1s,p1p,p1r,s1,r1)
    ds=trio(p2s,p2p,p2r,s2,r2)
    def pass_on(h,tr,own,recv,summed):
        tr[h][0].wait_recv()
        summed[h]=(own[h]+recv[h,0].astype(F32)).astype(BF)
        tr[h][2].start()
    for h in range(2): X[h,0]=hid[h*H:(h+1)*H]
    hc[0].wait_recv(); hf[0].start()
    loads[0].wait()
    hp[0].wait_recv(); hf[0].wait_recv()
    first(0)
    hc[1].wait_recv(); hf[1].start()
    loads[1].wait()
    second(0)
    cs[0][0].start(); cs[0][1].start()
    hp[1].wait_recv(); hf[1].wait_recv()
    first(1)
    pass_on(0,cs,p1c,p1r,p1p)
    second(1)
    cs[1][0].start(); cs[1][1].start()
    wait_bytes(feat,fsem.at[1])
    f=feat[...].astype(F32)
    mean=jnp.sum(jnp.sum(f,axis=0),axis=0,keepdims=True)*(1.0/C)
    sh=f-mean[None]
    var=jnp.sum(jnp.sum(sh*sh,axis=0),axis=0,keepdims=True)*(1.0/C)
    sh=sh*lax.rsqrt(var+1e-6)[None]
    nn=jnp.sum(jnp.sum(sh*sh,axis=0),axis=0,keepdims=True)
    sh=sh*lax.rsqrt(nn+1e-6)[None]
    target[...]=sh.reshape(C,T).T
    pass_on(1,cs,p1c,p1r,p1p)
    zc=[remote(Z.at[h,0],Z.at[h,2],zs.at[h],zr.at[h],cross) for h in range(2)]
    zp=[remote(Z.at[h,0],Z.at[h,1],zs.at[2+h],zr.at[2+h],partner) for h in range(2)]
    zf=[remote(Z.at[h,2],Z.at[h,3],zs.at[4+h],zr.at[4+h],partner) for h in range(2)]
    ii=lax.broadcasted_iota(jnp.int32,(H,T),0); jj=lax.broadcasted_iota(jnp.int32,(H,T),1)
    rows_of=[]
    def loss(h):
        cs[h][1].wait_recv(); cs[h][2].wait_recv()
        tg=target[h*H:(h+1)*H]
        pr=p1q[h]+p1r[h,1].astype(F32)+p1r[h,2].astype(F32)
        rinv=lax.rsqrt(jnp.sum(pr*pr,axis=1,keepdims=True)+1e-6)
        direction=pr*rinv
        cosine=jnp.sum(direction*tg,axis=1,keepdims=True)
        rows_of.append(jnp.sum(jnp.where(ii+h*H==jj,cosine,0.0),axis=0,keepdims=True))
        Z[h,0]=(-LOSS_WEIGHT*rinv*(tg-cosine*direction)).astype(BF)
        zc[h].start(); zp[h].start()
    loss(0)
    loss(1)
    cos_o[...]=rows_of[0]+rows_of[1]
    def slope(h):
        zp[h].wait_recv(); zf[h].wait_recv()
        def body(n,c):
            cols=pl.ds(pl.multiple_of(n*256,256),256)
            gs=dot_nt(Z[h].reshape(4*H,C),wo[cols,:])
            y=pre[h,:,cols]
            s=1.0/(1.0+jnp.exp(-y))
            sil[h,:,cols]=(gs*(s*(1.0+y*(1.0-s)))).astype(BF)
            return c
        lax.fori_loop(0,HID//256,body,0)
    def third(h):
        def part(cols):
            y=dot_nt(sil[h],wi[cols,:])
            p2q[h,:,cols]=y[:H]
            p2s[h,1,:,cols]=y[H:2*H].astype(BF)
            p2c[h,:,cols]=y[2*H:3*H]
            p2s[h,0,:,cols]=y[3*H:].astype(BF)
        def body(n,c):
            part(pl.ds(pl.multiple_of(n*256,256),256))
            return c
        lax.fori_loop(0,D//256,body,0)
        if D%256: part(pl.ds(D//256*256,D%256))
        ds[h][0].start(); ds[h][1].start()
    wait_bytes(xh,xsem.at[1])
    xcopy=pltpu.make_async_copy(xh,x_o,osem); xcopy.start()
    scores_prep(xh,kk,vt)
    zc[0].wait_recv(); zf[0].start()
    m=stage(0,xh,kk,vt,sa,None,None,None,None,first=True)
    zc[1].wait_recv(); zf[1].start()
    slope(0); third(0)
    m=pairs(0,1,m)
    pass_on(0,ds,p2c,p2r,p2p)
    slope(1); third(1)
    m=pairs(1,2,m)
    pass_on(1,ds,p2c,p2r,p2p)
    m=pairs(2,7,m)
    ucopy(0,0).wait()
    m=stage(NQ-1,xh,kk,vt,sb,sa,m,ua,a_o)
    ucopy(NQ-2,0).start()
    loads[2].wait()
    for h in range(2):
        ds[h][1].wait_recv(); ds[h][2].wait_recv()
        rows=pl.ds(h*H,H)
        gh[rows]=(cot[rows].astype(F32)+(p2q[h]+p2r[h,1].astype(F32)+p2r[h,2].astype(F32))).astype(BF)
    R=512
    def heads(i,c):
        at=lax.rem(seq//8+i,L//2//R)
        y=dot_nt(wa[pl.ds(pl.multiple_of(at*R,R),R)],gh[...]).astype(BF)
        gt[pl.ds(at*8,8)]=y.reshape(8,HD,T)
        for e in range(8):
            h=at*8+lax.rem(seq+e,8)
            @pl.when(h!=seq)
            def _():
                remote(gt.at[h],g_o.at[seq],gsem.at[0],gsem.at[1],(dp,h)).start()
            @pl.when(h==seq)
            def _():
                pltpu.make_async_copy(gt.at[h],g_o.at[seq],gsem.at[1]).start()
        return c
    lax.fori_loop(0,4,heads,0)
    ucopy(0,1).wait()
    stage(NQ,xh,kk,vt,None,sb,m,ub,a_o,last=True)
    ucopy(NQ-1,1).start()
    xcopy.wait()
    for n in range(2): ucopy(n,n).wait()
    for c in hc+hp+hf+zc+zp+zf+cs[0]+cs[1]+ds[0]+ds[1]: c.wait_send()
    wait_bytes(xt.at[pl.ds(0,NB-1)],xsem.at[0])
    wait_bytes(feat.at[pl.ds(0,NB-1)],fsem.at[0])
    wait_bytes(g_o,gsem.at[1]); wait_bytes(gt.at[pl.ds(0,NB-1)],gsem.at[0])


def front(hid,cot,q,k,v,wi,wo,wa,dino):
    vm=pl.BlockSpec(memory_space=pltpu.VMEM); hb=pl.BlockSpec(memory_space=pl.ANY)
    V=pltpu.VMEM; S=pltpu.SemaphoreType.DMA
    return pl.pallas_call(front_kernel,
        in_specs=[vm]*5+[hb]*3+[vm],out_specs=[vm,hb,hb,hb,vm],
        out_shape=[jax.ShapeDtypeStruct((1,T),F32),jax.ShapeDtypeStruct((NB,3*HD,T),BF),jax.ShapeDtypeStruct((NB,HD,T),BF),
            jax.ShapeDtypeStruct((NQ,L,QB),BF),jax.ShapeDtypeStruct((HD+16,L),F32)],
        scratch_shapes=[V((D,HID),BF),V((HID,C),BF),V((2048,D),BF),V((NB,3*HD,T),BF),V((NB,HD,T),BF),V((NB,48,T),BF),
            V((2,4,T//2,D),BF),V((2,4,T//2,C),BF),V((2,2*T,HID),F32),V((2,2*T,HID),BF),
            V((2,2,T//2,C),BF),V((2,T//2,C),F32),V((2,T//2,C),BF),V((2,3,T//2,C),BF),V((2,T//2,C),F32),
            V((2,2,T//2,D),BF),V((2,T//2,D),F32),V((2,T//2,D),BF),V((2,3,T//2,D),BF),V((2,T//2,D),F32),
            V((T,C),F32),V((T,D),BF),
            V((NB,3*HD,T),BF),V((L,T),BF),V((HD+16,L),BF),V((L,QB),F32),V((L,QB),F32),V((L,QB),BF),V((L,QB),BF),
            S((3,)),S((2,)),S((2,)),S((2,)),S((6,)),S((6,)),S((6,)),S((6,)),S((2,3)),S((2,3)),S((2,3)),S((2,3)),S((2,)),S],
        compiler_params=pltpu.CompilerParams(collective_id=0,has_side_effects=True,vmem_limit_bytes=62*2**20),
        name="front")(hid,cot,q,k,v,wi,wo,wa,dino)


def finish_kernel(x_ref,g_ref,a_ref,u_h,buf,vv,kt,ga,qn,gn,rlr,dq,u_ref,o_ref,usem,ksem,qsem):
    dp=lax.axis_index("dp"); seq=lax.axis_index("seq")
    NK=L//KB; per=KB//T
    first=seq//per
    def place(b): return lax.rem(b+first,NK)
    def fetch(b):
        slot=lax.rem(b,2)
        return pltpu.make_async_copy(u_h.at[:,pl.ds(pl.multiple_of(place(b)*KB,KB),KB)],u_ref.at[slot],usem.at[slot])
    fetch(0).start()
    greet(dp,seq,())
    grads_prep(x_ref,g_ref,a_ref,vv,kt,ga,qn,gn,rlr)
    dq[...]=jnp.zeros_like(dq)
    meet(0)
    def give(h,part,sem):
        @pl.when(h!=seq)
        def _():
            remote(o_ref.at[h,part],buf.at[seq,part],sem.at[0],sem.at[1],(dp,h)).start()
        @pl.when(h==seq)
        def _():
            pltpu.make_async_copy(o_ref.at[h,part],buf.at[seq,part],sem.at[1]).start()
    def body(b,c):
        slot=lax.rem(b,2)
        @pl.when(b<NK-1)
        def _(): fetch(b+1).start()
        fetch(b).wait()
        at=place(b)
        kr=pl.ds(pl.multiple_of(at*KB,KB),KB)
        v=vv[kr,:]; k=kt[:,kr]
        dk=jnp.zeros((KB,HD),F32); dv=jnp.zeros((KB,HD),F32)
        for i in range(L//QP):
            qr=pl.ds(i*QP,QP)
            n=QP//QB
            u=jnp.concatenate([u_ref[slot,i*n+e] for e in range(n)],axis=1)
            ds=(u.astype(F32)*dot(v,ga[:,qr])).astype(BF)
            dk=dk+dot(ds,qn[qr,:]); dv=dv+dot(u,gn[qr,:])
            dq[:,qr]+=dot(k,ds)
        for j in range(per):
            o_ref[at*per+j,HD:2*HD]=dk[j*T:(j+1)*T].T.astype(BF)
            o_ref[at*per+j,2*HD:]=dv[j*T:(j+1)*T].T.astype(BF)
        for j in range(per):
            give(at*per+lax.rem(seq+j,per),pl.ds(HD,2*HD),ksem)
        return c
    lax.fori_loop(0,NK,body,0)
    for j in range(NB):
        o_ref[j,:HD]=(dq[:,j*T:(j+1)*T]*rlr[0:1,j*T:(j+1)*T]).astype(BF)
    def send(r,c):
        give(lax.rem(seq+r,NB),pl.ds(0,HD),qsem)
        return c
    lax.fori_loop(0,NB,send,0)
    wait_bytes(buf.at[:,pl.ds(HD,2*HD)],ksem.at[1])
    wait_bytes(buf.at[:,pl.ds(0,HD)],qsem.at[1])
    wait_bytes(buf.at[pl.ds(0,NB-1),pl.ds(HD,2*HD)],ksem.at[0])
    wait_bytes(buf.at[pl.ds(0,NB-1),pl.ds(0,HD)],qsem.at[0])


def finish(x,g,u,a):
    V=pltpu.VMEM; S=pltpu.SemaphoreType.DMA
    vm=pl.BlockSpec(memory_space=V); hb=pl.BlockSpec(memory_space=pl.ANY)
    return pl.pallas_call(finish_kernel,in_specs=[vm]*3+[hb],out_specs=vm,
        out_shape=jax.ShapeDtypeStruct((NB,3*HD,T),BF),
        scratch_shapes=[V((L,T),BF),V((HD,L),BF),V((T,L),BF),V((L,HD),BF),V((L,HD),BF),V((8,L),F32),V((HD,L),F32),
            V((2,NQ,KB,QB),BF),V((NB,3*HD,T),BF),S((2,)),S((2,)),S((2,))],
        compiler_params=pltpu.CompilerParams(collective_id=1,has_side_effects=True,vmem_limit_bytes=56*2**20),
        name="finish")(x,g,a,u)


def place_kernel(o_ref,q_o,k_o,v_o):
    for n,ref in enumerate((q_o,k_o,v_o)):
        for p in range(o_ref.shape[0]//2):
            ref[:,p*T:(p+1)*T]=o_ref[2*p:2*p+2,n*HD:(n+1)*HD].reshape(T,T).T


def place(o):
    steps=2
    return pl.pallas_call(place_kernel,grid=(steps,),
        in_specs=[pl.BlockSpec((NB//steps,3*HD,T),lambda i:(i,0,0))],
        out_specs=[pl.BlockSpec((T,NB*HD//steps),lambda i:(0,i))]*3,
        out_shape=[jax.ShapeDtypeStruct((T,NB*HD),BF)]*3,name="place")(o)


def on_device(hidden,out_cot,proj_in,proj_out,attn_out_w,queries,keys,values,dino):
    cosine,x,g,u,a=front(hidden[0],out_cot[0],queries[0],keys[0],values[0],proj_in,proj_out,attn_out_w,dino[0])
    gq,gk,gv=place(finish(x,g,u,a))
    return cosine,gq[None],gk[None],gv[None]


def solution(mesh):
    in_specs = (
        P("dp", "seq", None),
        P("dp", "seq", None),
        P(None, "dp"),
        P("dp", None),
        P(),
        P("dp", "seq", None),
        P("dp", "seq", None),
        P("dp", "seq", None),
        P("dp", "seq", None),
    )
    out_specs = (P("dp", "seq"), P("dp", "seq", None), P("dp", "seq", None), P("dp", "seq", None))
    return jax.shard_map(
        on_device, mesh=mesh, in_specs=in_specs, out_specs=out_specs, check_vma=False
    )
```

```python
import jax
import jax.numpy as jnp
from jax import lax
from jax.experimental import pallas as pl
from jax.experimental.pallas import tpu as pltpu
from jax.sharding import PartitionSpec as P

LOG2E = 1.4426950408889634
F32=jnp.float32; BF=jnp.bfloat16
QB=256; KC=256; QP=512; KB=512; L=4096; NB=32; HD=64
T=128; D=2432; HID=1024; C=1536
NQ=L//QB
MESH=pl.DeviceIdType.MESH
LOSS_WEIGHT=1000.0

def dot(a,b): return jnp.dot(a,b,preferred_element_type=F32)
def dot_nt(a,b): return lax.dot_general(a,b,(((1,),(1,)),((),())),preferred_element_type=F32)

def scores_prep(x,kk,vt):
    for j in range(NB):
        rows=pl.ds(j*T,T)
        kn=x[j,HD:2*HD].T
        kk[rows,:]=jnp.concatenate([kn,kn],axis=1)
        vt[pl.ds(0,HD),rows]=x[j,2*HD:]
    vt[pl.ds(HD,16),:]=jnp.ones((16,L),BF)


def stage(i,x,kk,vt,sn,so,m,u_ref,a_ref,first=False,last=False):
    per=QB//T
    if not last:
        qt=jnp.concatenate([x[i*per+j,:HD] for j in range(per)],axis=1)
        qf=qt.astype(F32)*(0.125*LOG2E)
        qhi=qf.astype(BF); qlo=(qf-qhi.astype(F32)).astype(BF)
        qa=jnp.concatenate([qhi,qlo],axis=0)
    mn=jnp.full((8,QB),-jnp.inf,F32)
    acc=jnp.zeros((HD+16,QB),F32)
    for c in range(L//KC):
        rows=pl.ds(c*KC,KC)
        if not last:
            y=dot(kk[rows,:],qa)
            sn[rows,:]=y
            mn=jnp.maximum(mn,jnp.max(y.reshape(KC//8,8,QB),axis=0))
        if not first:
            u=jnp.exp2(so[rows,:]-m).astype(BF)
            u_ref[rows,:]=u
            acc=acc+dot(vt[:,rows],u)
    if not first:
        j=i-1
        a_ref[:,pl.ds(j*QB if isinstance(j,int) else pl.multiple_of(j*QB,QB),QB)]=acc
    return jnp.max(mn,axis=0,keepdims=True)


def grads_prep(lo,hi,x,g_ref,a_ref,vv,kt,ga,qn,gn,rlr):
    lane=lax.broadcasted_iota(jnp.int32,(T,HD),1)
    ones=jnp.where(lane<2,1.0,0.0).astype(BF)
    row=lax.broadcasted_iota(jnp.int32,(HD,T),0)
    for j in range(lo,hi):
        rows=pl.ds(j*T,T)
        vv[rows,:]=jnp.concatenate([x[j,2*HD:].T,ones],axis=1)
        kt[:,rows]=x[j,HD:2*HD]*BF(0.125)
        a=a_ref[:,rows]
        rl=1.0/a[HD:HD+1]
        rlr[0:1,rows]=rl
        gt=g_ref[j]; gf=gt.astype(F32)
        d=-jnp.sum(gf*a[:HD],axis=0,keepdims=True)*rl
        dhi=d.astype(BF); dlo=d-dhi.astype(F32)
        ga[pl.ds(0,HD),rows]=gt
        ga[pl.ds(HD,HD),rows]=jnp.where(row==0,dhi.astype(F32),jnp.where(row==1,dlo,0.0)).astype(BF)
        qn[rows,:]=(x[j,:HD].astype(F32)*(rl*0.125)).T.astype(BF)
        gn[rows,:]=(gf*rl).T.astype(BF)


def remote(src,dst,send,recv,dev):
    return pltpu.make_async_remote_copy(src_ref=src,dst_ref=dst,send_sem=send,recv_sem=recv,device_id=dev,device_id_type=MESH)


def wait_bytes(ref,sem):
    pltpu.make_async_copy(ref,ref,sem).wait()


def greet(dp,seq,extra):
    barrier=pltpu.get_barrier_semaphore()
    def hello(r,c):
        pl.semaphore_signal(barrier,inc=1,device_id=(dp,lax.rem(seq+r,NB)),device_id_type=MESH)
        return c
    lax.fori_loop(1,NB,hello,0)
    for dev in extra:
        pl.semaphore_signal(barrier,inc=1,device_id=dev,device_id_type=MESH)


def meet(extra):
    pl.semaphore_wait(pltpu.get_barrier_semaphore(),NB-1+extra)


def front_kernel(hid,cot,q,k,v,wi_h,wo_h,wa_h,dino, cos_o,x_o,g_o,u_o,a_o,
        wi,wo,wa,xt,gt,feat,X,Z,pre,sil,p1s,p1c,p1p,p1r,p1q,p2s,p2c,p2p,p2r,p2q,target,gh,
        xh,kk,vt,sa,sb,ua,ub,wsem,xsem,fsem,gsem,hs,hr,zs,zr,s1,r1,s2,r2,usem,osem):
    dp=lax.axis_index("dp"); seq=lax.axis_index("seq")
    core=lax.rem(dp,2); hi=dp//2
    partner=(hi*2+(1-core),seq)
    cross_seq=lax.rem(seq+NB//2,NB)
    cross=((1-hi)*2+core,cross_seq)
    diag=((1-hi)*2+(1-core),cross_seq)
    loads=[pltpu.make_async_copy(a,b,wsem.at[n]) for n,(a,b) in enumerate(((wi_h,wi),(wo_h,wo),(wa_h,wa)))]
    for ld in loads: ld.start()
    greet(dp,seq,(partner,cross))
    meet(2)
    H=T//2
    def ucopy(i,n): return pltpu.make_async_copy((ua,ub)[n],u_o.at[i],usem.at[n])
    def pairs(lo,hi_,m):
        def body(p,m):
            i=2*p+1
            @pl.when(p>0)
            def _(): ucopy(0,0).wait()
            m=stage(i,xh,kk,vt,sb,sa,m,ua,a_o)
            ucopy(i-1,0).start()
            @pl.when(p>0)
            def _(): ucopy(0,1).wait()
            m=stage(i+1,xh,kk,vt,sa,sb,m,ub,a_o)
            ucopy(i,1).start()
            return m
        return lax.fori_loop(lo,hi_,body,m)
    hc=[remote(hid.at[pl.ds(h*H,H)],X.at[h,2],hs.at[h],hr.at[h],cross) for h in range(2)]
    hp=[remote(hid.at[pl.ds(h*H,H)],X.at[h,1],hs.at[2+h],hr.at[2+h],partner) for h in range(2)]
    hf=[remote(X.at[h,2],X.at[h,3],hs.at[4+h],hr.at[4+h],partner) for h in range(2)]
    hc[0].start(); hp[0].start(); hc[1].start(); hp[1].start()
    def send_feat(r,c):
        peer=lax.rem(seq+r,NB)
        remote(dino.at[:,pl.ds(pl.multiple_of(peer*T,T),T)],feat.at[seq],fsem.at[0],fsem.at[1],(dp,peer)).start()
        return c
    pltpu.make_async_copy(dino.at[:,pl.ds(pl.multiple_of(seq*T,T),T)],feat.at[seq],fsem.at[1]).start()
    lax.fori_loop(1,NB,send_feat,0)
    def turn(p):
        cols=pl.ds(pl.multiple_of(p*T,T),T)
        for n,ref in enumerate((q,k,v)):
            t=ref[:,cols].T
            xt[2*p,pl.ds(n*HD,HD)]=t[:HD]
            xt[2*p+1,pl.ds(n*HD,HD)]=t[HD:]
    base=seq//2
    turn(base)
    pltpu.make_async_copy(xt.at[seq],xh.at[seq],xsem.at[1]).start()
    mate=base*2+(1-lax.rem(seq,2))
    remote(xt.at[mate],xh.at[seq],xsem.at[0],xsem.at[1],(dp,mate)).start()
    def turn_send(i,c):
        p=lax.rem(base+i,NB//2)
        turn(p)
        for e in range(2):
            remote(xt.at[2*p+e],xh.at[seq],xsem.at[0],xsem.at[1],(dp,2*p+e)).start()
        return c
    lax.fori_loop(1,NB//2,turn_send,0)
    def first(h):
        def body(n,c):
            cols=pl.ds(pl.multiple_of(n*256,256),256)
            y=dot(X[h].reshape(4*H,D),wi[:,cols])
            pre[h,:,cols]=y
            sil[h,:,cols]=(y/(1.0+jnp.exp(-y))).astype(BF)
            return c
        lax.fori_loop(0,HID//256,body,0)
    def second(h):
        def body(n,c):
            cols=pl.ds(pl.multiple_of(n*256,256),256)
            y=dot(sil[h],wo[:,cols])
            p1q[h,:,cols]=y[:H]
            p1s[h,1,:,cols]=y[H:2*H].astype(BF)
            p1c[h,:,cols]=y[2*H:3*H]
            p1s[h,0,:,cols]=y[3*H:].astype(BF)
            return c
        lax.fori_loop(0,C//256,body,0)
    def trio(sent,summed,recv,ss,rs):
        return [[remote(sent.at[h,0],recv.at[h,0],ss.at[h,0],rs.at[h,0],partner),
            remote(sent.at[h,1],recv.at[h,1],ss.at[h,1],rs.at[h,1],partner),
            remote(summed.at[h],recv.at[h,2],ss.at[h,2],rs.at[h,2],cross)] for h in range(2)]
    cs=trio(p1s,p1p,p1r,s1,r1)
    ds=trio(p2s,p2p,p2r,s2,r2)
    def pass_on(h,tr,own,recv,summed):
        tr[h][0].wait_recv()
        summed[h]=(own[h]+recv[h,0].astype(F32)).astype(BF)
        tr[h][2].start()
    for h in range(2): X[h,0]=hid[h*H:(h+1)*H]
    hc[0].wait_recv(); hf[0].start()
    loads[0].wait()
    hp[0].wait_recv(); hf[0].wait_recv()
    first(0)
    hc[1].wait_recv(); hf[1].start()
    loads[1].wait()
    second(0)
    cs[0][0].start(); cs[0][1].start()
    hp[1].wait_recv(); hf[1].wait_recv()
    first(1)
    pass_on(0,cs,p1c,p1r,p1p)
    second(1)
    cs[1][0].start(); cs[1][1].start()
    wait_bytes(feat,fsem.at[1])
    f=feat[...].astype(F32)
    mean=jnp.sum(jnp.sum(f,axis=0),axis=0,keepdims=True)*(1.0/C)
    sh=f-mean[None]
    var=jnp.sum(jnp.sum(sh*sh,axis=0),axis=0,keepdims=True)*(1.0/C)
    sh=sh*lax.rsqrt(var+1e-6)[None]
    nn=jnp.sum(jnp.sum(sh*sh,axis=0),axis=0,keepdims=True)
    sh=sh*lax.rsqrt(nn+1e-6)[None]
    target[...]=sh.reshape(C,T).T
    pass_on(1,cs,p1c,p1r,p1p)
    zc=[remote(Z.at[h,0],Z.at[h,2],zs.at[h],zr.at[h],cross) for h in range(2)]
    zp=[remote(Z.at[h,0],Z.at[h,1],zs.at[2+h],zr.at[2+h],partner) for h in range(2)]
    zf=[remote(Z.at[h,2],Z.at[h,3],zs.at[4+h],zr.at[4+h],partner) for h in range(2)]
    ii=lax.broadcasted_iota(jnp.int32,(H,T),0); jj=lax.broadcasted_iota(jnp.int32,(H,T),1)
    rows_of=[]
    def loss(h):
        cs[h][1].wait_recv(); cs[h][2].wait_recv()
        tg=target[h*H:(h+1)*H]
        pr=p1q[h]+p1r[h,1].astype(F32)+p1r[h,2].astype(F32)
        rinv=lax.rsqrt(jnp.sum(pr*pr,axis=1,keepdims=True)+1e-6)
        direction=pr*rinv
        cosine=jnp.sum(direction*tg,axis=1,keepdims=True)
        rows_of.append(jnp.sum(jnp.where(ii+h*H==jj,cosine,0.0),axis=0,keepdims=True))
        Z[h,0]=(-LOSS_WEIGHT*rinv*(tg-cosine*direction)).astype(BF)
        zc[h].start(); zp[h].start()
    loss(0)
    loss(1)
    cos_o[...]=rows_of[0]+rows_of[1]
    def slope(h):
        zp[h].wait_recv(); zf[h].wait_recv()
        def body(n,c):
            cols=pl.ds(pl.multiple_of(n*256,256),256)
            gs=dot_nt(Z[h].reshape(4*H,C),wo[cols,:])
            y=pre[h,:,cols]
            s=1.0/(1.0+jnp.exp(-y))
            sil[h,:,cols]=(gs*(s*(1.0+y*(1.0-s)))).astype(BF)
            return c
        lax.fori_loop(0,HID//256,body,0)
    def third(h):
        def part(cols):
            y=dot_nt(sil[h],wi[cols,:])
            p2q[h,:,cols]=y[:H]
            p2s[h,1,:,cols]=y[H:2*H].astype(BF)
            p2c[h,:,cols]=y[2*H:3*H]
            p2s[h,0,:,cols]=y[3*H:].astype(BF)
        def body(n,c):
            part(pl.ds(pl.multiple_of(n*256,256),256))
            return c
        lax.fori_loop(0,D//256,body,0)
        if D%256: part(pl.ds(D//256*256,D%256))
        ds[h][0].start(); ds[h][1].start()
    wait_bytes(xh,xsem.at[1])
    xcopy=pltpu.make_async_copy(xh,x_o,osem); xcopy.start()
    scores_prep(xh,kk,vt)
    zc[0].wait_recv(); zf[0].start()
    m=stage(0,xh,kk,vt,sa,None,None,None,None,first=True)
    zc[1].wait_recv(); zf[1].start()
    slope(0); third(0)
    m=pairs(0,1,m)
    pass_on(0,ds,p2c,p2r,p2p)
    slope(1); third(1)
    m=pairs(1,2,m)
    pass_on(1,ds,p2c,p2r,p2p)
    m=pairs(2,4,m)
    loads[2].wait()
    for h in range(2):
        ds[h][1].wait_recv(); ds[h][2].wait_recv()
        rows=pl.ds(h*H,H)
        gh[rows]=(cot[rows].astype(F32)+(p2q[h]+p2r[h,1].astype(F32)+p2r[h,2].astype(F32))).astype(BF)
    R=512
    def heads(i,c):
        at=lax.rem(seq//8+i,L//2//R)
        y=dot_nt(wa[pl.ds(pl.multiple_of(at*R,R),R)],gh[...]).astype(BF)
        gt[pl.ds(at*8,8)]=y.reshape(8,HD,T)
        for e in range(8):
            h=at*8+lax.rem(seq+e,8)
            @pl.when(h!=seq)
            def _():
                remote(gt.at[h],g_o.at[seq],gsem.at[0],gsem.at[1],(dp,h)).start()
            @pl.when(h==seq)
            def _():
                pltpu.make_async_copy(gt.at[h],g_o.at[seq],gsem.at[1]).start()
        return c
    lax.fori_loop(0,4,heads,0)
    m=pairs(4,7,m)
    ucopy(0,0).wait()
    m=stage(NQ-1,xh,kk,vt,sb,sa,m,ua,a_o)
    ucopy(NQ-2,0).start()
    ucopy(0,1).wait()
    stage(NQ,xh,kk,vt,None,sb,m,ub,a_o,last=True)
    ucopy(NQ-1,1).start()
    xcopy.wait()
    for n in range(2): ucopy(n,n).wait()
    for c in hc+hp+hf+zc+zp+zf+cs[0]+cs[1]+ds[0]+ds[1]: c.wait_send()
    wait_bytes(xt.at[pl.ds(0,NB-1)],xsem.at[0])
    wait_bytes(feat.at[pl.ds(0,NB-1)],fsem.at[0])
    wait_bytes(g_o,gsem.at[1]); wait_bytes(gt.at[pl.ds(0,NB-1)],gsem.at[0])


def front(hid,cot,q,k,v,wi,wo,wa,dino):
    vm=pl.BlockSpec(memory_space=pltpu.VMEM); hb=pl.BlockSpec(memory_space=pl.ANY)
    V=pltpu.VMEM; S=pltpu.SemaphoreType.DMA
    return pl.pallas_call(front_kernel,
        in_specs=[vm]*5+[hb]*3+[vm],out_specs=[vm,hb,hb,hb,vm],
        out_shape=[jax.ShapeDtypeStruct((1,T),F32),jax.ShapeDtypeStruct((NB,3*HD,T),BF),jax.ShapeDtypeStruct((NB,HD,T),BF),
            jax.ShapeDtypeStruct((NQ,L,QB),BF),jax.ShapeDtypeStruct((HD+16,L),F32)],
        scratch_shapes=[V((D,HID),BF),V((HID,C),BF),V((2048,D),BF),V((NB,3*HD,T),BF),V((NB,HD,T),BF),V((NB,48,T),BF),
            V((2,4,T//2,D),BF),V((2,4,T//2,C),BF),V((2,2*T,HID),F32),V((2,2*T,HID),BF),
            V((2,2,T//2,C),BF),V((2,T//2,C),F32),V((2,T//2,C),BF),V((2,3,T//2,C),BF),V((2,T//2,C),F32),
            V((2,2,T//2,D),BF),V((2,T//2,D),F32),V((2,T//2,D),BF),V((2,3,T//2,D),BF),V((2,T//2,D),F32),
            V((T,C),F32),V((T,D),BF),
            V((NB,3*HD,T),BF),V((L,T),BF),V((HD+16,L),BF),V((L,QB),F32),V((L,QB),F32),V((L,QB),BF),V((L,QB),BF),
            S((3,)),S((2,)),S((2,)),S((2,)),S((6,)),S((6,)),S((6,)),S((6,)),S((2,3)),S((2,3)),S((2,3)),S((2,3)),S((2,)),S],
        compiler_params=pltpu.CompilerParams(collective_id=0,has_side_effects=True,vmem_limit_bytes=62*2**20),
        name="front")(hid,cot,q,k,v,wi,wo,wa,dino)


def finish_kernel(x_ref,g_ref,a_ref,u_h,buf,vv,kt,ga,qn,gn,rlr,dq,u_ref,o_ref,usem,ksem,qsem):
    dp=lax.axis_index("dp"); seq=lax.axis_index("seq")
    NK=L//KB; per=KB//T
    first=seq//per
    way=1-2*lax.rem(seq,2)
    def place(b): return lax.rem(first+way*(b+1)+2*NK,NK)
    def fetch(b):
        slot=lax.rem(b,2)
        return pltpu.make_async_copy(u_h.at[:,pl.ds(pl.multiple_of(place(b)*KB,KB),KB)],u_ref.at[slot],usem.at[slot])
    fetch(0).start()
    greet(dp,seq,())
    def prep(i):
        grads_prep(i*QP//T,(i+1)*QP//T,x_ref,g_ref,a_ref,vv,kt,ga,qn,gn,rlr)
    def give(h,part,sem):
        @pl.when(h!=seq)
        def _():
            remote(o_ref.at[h,part],buf.at[seq,part],sem.at[0],sem.at[1],(dp,h)).start()
        @pl.when(h==seq)
        def _():
            pltpu.make_async_copy(o_ref.at[h,part],buf.at[seq,part],sem.at[1]).start()
    def block(b,at,v,k,start):
        slot=lax.rem(b,2)
        dk=jnp.zeros((KB,HD),F32); dv=jnp.zeros((KB,HD),F32)
        for i in range(L//QP):
            if start and i+1<L//QP: prep(i+1)
            qr=pl.ds(i*QP,QP)
            n=QP//QB
            u=jnp.concatenate([u_ref[slot,i*n+e] for e in range(n)],axis=1)
            ds=(u.astype(F32)*dot(v,ga[:,qr])).astype(BF)
            dk=dk+dot(ds,qn[qr,:]); dv=dv+dot(u,gn[qr,:])
            part=dot(k,ds)
            if start: dq[:,qr]=part
            else: dq[:,qr]+=part
        for j in range(per):
            o_ref[at*per+j,HD:2*HD]=dk[j*T:(j+1)*T].T.astype(BF)
            o_ref[at*per+j,2*HD:]=dv[j*T:(j+1)*T].T.astype(BF)
        if start: meet(0)
        for j in range(per):
            give(at*per+lax.rem(seq+j,per),pl.ds(HD,2*HD),ksem)
    prep(0)
    at=place(0)
    lane=lax.broadcasted_iota(jnp.int32,(T,HD),1)
    ones=jnp.where(lane<2,1.0,0.0).astype(BF)
    v=jnp.concatenate([jnp.concatenate([x_ref[at*per+j,2*HD:].T,ones],axis=1) for j in range(per)],axis=0)
    k=jnp.concatenate([x_ref[at*per+j,HD:2*HD]*BF(0.125) for j in range(per)],axis=1)
    fetch(1).start()
    fetch(0).wait()
    block(0,at,v,k,True)
    def body(b,c):
        @pl.when(b<NK-1)
        def _(): fetch(b+1).start()
        fetch(b).wait()
        at=place(b)
        kr=pl.ds(pl.multiple_of(at*KB,KB),KB)
        block(b,at,vv[kr,:],kt[:,kr],False)
        return c
    lax.fori_loop(1,NK,body,0)
    for j in range(NB):
        o_ref[j,:HD]=(dq[:,j*T:(j+1)*T]*rlr[0:1,j*T:(j+1)*T]).astype(BF)
    def send(r,c):
        give(lax.rem(seq+r,NB),pl.ds(0,HD),qsem)
        return c
    lax.fori_loop(0,NB,send,0)
    wait_bytes(buf.at[:,pl.ds(HD,2*HD)],ksem.at[1])
    wait_bytes(buf.at[:,pl.ds(0,HD)],qsem.at[1])
    wait_bytes(buf.at[pl.ds(0,NB-1),pl.ds(HD,2*HD)],ksem.at[0])
    wait_bytes(buf.at[pl.ds(0,NB-1),pl.ds(0,HD)],qsem.at[0])


def finish(x,g,u,a):
    V=pltpu.VMEM; S=pltpu.SemaphoreType.DMA
    vm=pl.BlockSpec(memory_space=V); hb=pl.BlockSpec(memory_space=pl.ANY)
    return pl.pallas_call(finish_kernel,in_specs=[vm]*3+[hb],out_specs=vm,
        out_shape=jax.ShapeDtypeStruct((NB,3*HD,T),BF),
        scratch_shapes=[V((L,T),BF),V((HD,L),BF),V((T,L),BF),V((L,HD),BF),V((L,HD),BF),V((8,L),F32),V((HD,L),F32),
            V((2,NQ,KB,QB),BF),V((NB,3*HD,T),BF),S((2,)),S((2,)),S((2,))],
        compiler_params=pltpu.CompilerParams(collective_id=1,has_side_effects=True,vmem_limit_bytes=56*2**20),
        name="finish")(x,g,a,u)


def place_kernel(o_ref,q_o,k_o,v_o):
    for n,ref in enumerate((q_o,k_o,v_o)):
        for p in range(o_ref.shape[0]//2):
            ref[:,p*T:(p+1)*T]=o_ref[2*p:2*p+2,n*HD:(n+1)*HD].reshape(T,T).T


def place(o):
    steps=2
    return pl.pallas_call(place_kernel,grid=(steps,),
        in_specs=[pl.BlockSpec((NB//steps,3*HD,T),lambda i:(i,0,0))],
        out_specs=[pl.BlockSpec((T,NB*HD//steps),lambda i:(0,i))]*3,
        out_shape=[jax.ShapeDtypeStruct((T,NB*HD),BF)]*3,name="place")(o)


def on_device(hidden,out_cot,proj_in,proj_out,attn_out_w,queries,keys,values,dino):
    cosine,x,g,u,a=front(hidden[0],out_cot[0],queries[0],keys[0],values[0],proj_in,proj_out,attn_out_w,dino[0])
    gq,gk,gv=place(finish(x,g,u,a))
    return cosine,gq[None],gk[None],gv[None]


def solution(mesh):
    in_specs = (
        P("dp", "seq", None),
        P("dp", "seq", None),
        P(None, "dp"),
        P("dp", None),
        P(),
        P("dp", "seq", None),
        P("dp", "seq", None),
        P("dp", "seq", None),
        P("dp", "seq", None),
    )
    out_specs = (P("dp", "seq"), P("dp", "seq", None), P("dp", "seq", None), P("dp", "seq", None))
    return jax.shard_map(
        on_device, mesh=mesh, in_specs=in_specs, out_specs=out_specs, check_vma=False
    )
```

```python
import jax
import jax.numpy as jnp
from jax import lax
from jax.experimental import pallas as pl
from jax.experimental.pallas import tpu as pltpu
from jax.sharding import PartitionSpec as P

LOG2E = 1.4426950408889634
F32=jnp.float32; BF=jnp.bfloat16
QB=256; KC=256; QP=512; KB=512; L=4096; NB=32; HD=64
T=128; D=2432; HID=1024; C=1536
NQ=L//QB
MESH=pl.DeviceIdType.MESH
LOSS_WEIGHT=1000.0

def dot(a,b): return jnp.dot(a,b,preferred_element_type=F32)
def dot_nt(a,b): return lax.dot_general(a,b,(((1,),(1,)),((),())),preferred_element_type=F32)

def scores_prep(x,kk,vt):
    for j in range(NB):
        rows=pl.ds(j*T,T)
        kn=x[j,HD:2*HD].T
        kk[rows,:]=jnp.concatenate([kn,kn],axis=1)
        vt[pl.ds(0,HD),rows]=x[j,2*HD:]
    vt[pl.ds(HD,16),:]=jnp.ones((16,L),BF)


def stage(i,x,kk,vt,sn,so,m,u_ref,a_ref,first=False,last=False):
    per=QB//T
    if not last:
        qt=jnp.concatenate([x[i*per+j,:HD] for j in range(per)],axis=1)
        qf=qt.astype(F32)*(0.125*LOG2E)
        qhi=qf.astype(BF); qlo=(qf-qhi.astype(F32)).astype(BF)
        qa=jnp.concatenate([qhi,qlo],axis=0)
    mn=jnp.full((8,QB),-jnp.inf,F32)
    acc=jnp.zeros((HD+16,QB),F32)
    for c in range(L//KC):
        rows=pl.ds(c*KC,KC)
        if not last:
            y=dot(kk[rows,:],qa)
            sn[rows,:]=y
            mn=jnp.maximum(mn,jnp.max(y.reshape(KC//8,8,QB),axis=0))
        if not first:
            u=jnp.exp2(so[rows,:]-m).astype(BF)
            u_ref[rows,:]=u
            acc=acc+dot(vt[:,rows],u)
    if not first:
        j=i-1
        a_ref[:,pl.ds(j*QB if isinstance(j,int) else pl.multiple_of(j*QB,QB),QB)]=acc
    return jnp.max(mn,axis=0,keepdims=True)


def grads_prep(lo,hi,x,g_ref,a_ref,vv,kt,ga,qn,gn,rlr):
    lane=lax.broadcasted_iota(jnp.int32,(T,HD),1)
    ones=jnp.where(lane<2,1.0,0.0).astype(BF)
    row=lax.broadcasted_iota(jnp.int32,(HD,T),0)
    for j in range(lo,hi):
        rows=pl.ds(j*T,T)
        vv[rows,:]=jnp.concatenate([x[j,2*HD:].T,ones],axis=1)
        kt[:,rows]=x[j,HD:2*HD]*BF(0.125)
        a=a_ref[:,rows]
        rl=1.0/a[HD:HD+1]
        rlr[0:1,rows]=rl
        gt=g_ref[j]; gf=gt.astype(F32)
        d=-jnp.sum(gf*a[:HD],axis=0,keepdims=True)*rl
        dhi=d.astype(BF); dlo=d-dhi.astype(F32)
        ga[pl.ds(0,HD),rows]=gt
        ga[pl.ds(HD,HD),rows]=jnp.where(row==0,dhi.astype(F32),jnp.where(row==1,dlo,0.0)).astype(BF)
        qn[rows,:]=(x[j,:HD].astype(F32)*(rl*0.125)).T.astype(BF)
        gn[rows,:]=(gf*rl).T.astype(BF)


def remote(src,dst,send,recv,dev):
    return pltpu.make_async_remote_copy(src_ref=src,dst_ref=dst,send_sem=send,recv_sem=recv,device_id=dev,device_id_type=MESH)


def wait_bytes(ref,sem):
    pltpu.make_async_copy(ref,ref,sem).wait()


def greet(dp,seq,extra):
    barrier=pltpu.get_barrier_semaphore()
    def hello(r,c):
        pl.semaphore_signal(barrier,inc=1,device_id=(dp,lax.rem(seq+r,NB)),device_id_type=MESH)
        return c
    lax.fori_loop(1,NB,hello,0)
    for dev in extra:
        pl.semaphore_signal(barrier,inc=1,device_id=dev,device_id_type=MESH)


def meet(extra):
    pl.semaphore_wait(pltpu.get_barrier_semaphore(),NB-1+extra)


def front_kernel(hid,cot,q,k,v,wi_h,wo_h,wa_h,dino, cos_o,x_o,g_o,u_o,a_o,
        wi,wo,wa,xt,gt,feat,X,Z,pre,sil,p1s,p1c,p1p,p1r,p1q,p2s,p2c,p2p,p2r,p2q,target,gh,
        xh,kk,vt,sa,sb,ua,ub,wsem,xsem,fsem,gsem,hs,hr,zs,zr,s1,r1,s2,r2,usem,osem):
    dp=lax.axis_index("dp"); seq=lax.axis_index("seq")
    core=lax.rem(dp,2); hi=dp//2
    partner=(hi*2+(1-core),seq)
    cross_seq=lax.rem(seq+NB//2,NB)
    cross=((1-hi)*2+core,cross_seq)
    diag=((1-hi)*2+(1-core),cross_seq)
    loads=[pltpu.make_async_copy(a,b,wsem.at[n]) for n,(a,b) in enumerate(((wi_h,wi),(wo_h,wo),(wa_h,wa)))]
    for ld in loads: ld.start()
    greet(dp,seq,(partner,cross))
    meet(2)
    H=T//2
    def ucopy(i,n): return pltpu.make_async_copy((ua,ub)[n],u_o.at[i],usem.at[n])
    def pairs(lo,hi_,m):
        def body(p,m):
            i=2*p+1
            @pl.when(p>0)
            def _(): ucopy(0,0).wait()
            m=stage(i,xh,kk,vt,sb,sa,m,ua,a_o)
            ucopy(i-1,0).start()
            @pl.when(p>0)
            def _(): ucopy(0,1).wait()
            m=stage(i+1,xh,kk,vt,sa,sb,m,ub,a_o)
            ucopy(i,1).start()
            return m
        return lax.fori_loop(lo,hi_,body,m)
    hc=[remote(hid.at[pl.ds(h*H,H)],X.at[h,2],hs.at[h],hr.at[h],cross) for h in range(2)]
    hp=[remote(hid.at[pl.ds(h*H,H)],X.at[h,1],hs.at[2+h],hr.at[2+h],partner) for h in range(2)]
    hf=[remote(X.at[h,2],X.at[h,3],hs.at[4+h],hr.at[4+h],partner) for h in range(2)]
    hc[0].start(); hp[0].start(); hc[1].start(); hp[1].start()
    def send_feat(r,c):
        peer=lax.rem(seq+r,NB)
        remote(dino.at[:,pl.ds(pl.multiple_of(peer*T,T),T)],feat.at[seq],fsem.at[0],fsem.at[1],(dp,peer)).start()
        return c
    pltpu.make_async_copy(dino.at[:,pl.ds(pl.multiple_of(seq*T,T),T)],feat.at[seq],fsem.at[1]).start()
    lax.fori_loop(1,NB,send_feat,0)
    def turn(p):
        cols=pl.ds(pl.multiple_of(p*T,T),T)
        for n,ref in enumerate((q,k,v)):
            t=ref[:,cols].T
            xt[2*p,pl.ds(n*HD,HD)]=t[:HD]
            xt[2*p+1,pl.ds(n*HD,HD)]=t[HD:]
    base=seq//2
    turn(base)
    pltpu.make_async_copy(xt.at[seq],xh.at[seq],xsem.at[1]).start()
    mate=base*2+(1-lax.rem(seq,2))
    remote(xt.at[mate],xh.at[seq],xsem.at[0],xsem.at[1],(dp,mate)).start()
    def turn_send(i,c):
        p=lax.rem(base+i,NB//2)
        turn(p)
        for e in range(2):
            remote(xt.at[2*p+e],xh.at[seq],xsem.at[0],xsem.at[1],(dp,2*p+e)).start()
        return c
    lax.fori_loop(1,NB//2,turn_send,0)
    def first(h):
        def body(n,c):
            cols=pl.ds(pl.multiple_of(n*256,256),256)
            y=dot(X[h].reshape(4*H,D),wi[:,cols])
            pre[h,:,cols]=y
            sil[h,:,cols]=(y/(1.0+jnp.exp(-y))).astype(BF)
            return c
        lax.fori_loop(0,HID//256,body,0)
    def second(h):
        def body(n,c):
            cols=pl.ds(pl.multiple_of(n*256,256),256)
            y=dot(sil[h],wo[:,cols])
            p1q[h,:,cols]=y[:H]
            p1s[h,1,:,cols]=y[H:2*H].astype(BF)
            p1c[h,:,cols]=y[2*H:3*H]
            p1s[h,0,:,cols]=y[3*H:].astype(BF)
            return c
        lax.fori_loop(0,C//256,body,0)
    def trio(sent,summed,recv,ss,rs):
        return [[remote(sent.at[h,0],recv.at[h,0],ss.at[h,0],rs.at[h,0],partner),
            remote(sent.at[h,1],recv.at[h,1],ss.at[h,1],rs.at[h,1],partner),
            remote(summed.at[h],recv.at[h,2],ss.at[h,2],rs.at[h,2],cross)] for h in range(2)]
    cs=trio(p1s,p1p,p1r,s1,r1)
    ds=trio(p2s,p2p,p2r,s2,r2)
    def pass_on(h,tr,own,recv,summed):
        tr[h][0].wait_recv()
        summed[h]=(own[h]+recv[h,0].astype(F32)).astype(BF)
        tr[h][2].start()
    for h in range(2): X[h,0]=hid[h*H:(h+1)*H]
    hc[0].wait_recv(); hf[0].start()
    loads[0].wait()
    hp[0].wait_recv(); hf[0].wait_recv()
    first(0)
    hc[1].wait_recv(); hf[1].start()
    loads[1].wait()
    second(0)
    cs[0][0].start(); cs[0][1].start()
    hp[1].wait_recv(); hf[1].wait_recv()
    first(1)
    pass_on(0,cs,p1c,p1r,p1p)
    second(1)
    cs[1][0].start(); cs[1][1].start()
    wait_bytes(feat,fsem.at[1])
    f=feat[...].astype(F32)
    mean=jnp.sum(jnp.sum(f,axis=0),axis=0,keepdims=True)*(1.0/C)
    sh=f-mean[None]
    var=jnp.sum(jnp.sum(sh*sh,axis=0),axis=0,keepdims=True)*(1.0/C)
    sh=sh*lax.rsqrt(var+1e-6)[None]
    nn=jnp.sum(jnp.sum(sh*sh,axis=0),axis=0,keepdims=True)
    sh=sh*lax.rsqrt(nn+1e-6)[None]
    target[...]=sh.reshape(C,T).T
    pass_on(1,cs,p1c,p1r,p1p)
    zc=[remote(Z.at[h,0],Z.at[h,2],zs.at[h],zr.at[h],cross) for h in range(2)]
    zp=[remote(Z.at[h,0],Z.at[h,1],zs.at[2+h],zr.at[2+h],partner) for h in range(2)]
    zf=[remote(Z.at[h,2],Z.at[h,3],zs.at[4+h],zr.at[4+h],partner) for h in range(2)]
    ii=lax.broadcasted_iota(jnp.int32,(H,T),0); jj=lax.broadcasted_iota(jnp.int32,(H,T),1)
    rows_of=[]
    def loss(h):
        cs[h][1].wait_recv(); cs[h][2].wait_recv()
        tg=target[h*H:(h+1)*H]
        pr=p1q[h]+p1r[h,1].astype(F32)+p1r[h,2].astype(F32)
        rinv=lax.rsqrt(jnp.sum(pr*pr,axis=1,keepdims=True)+1e-6)
        direction=pr*rinv
        cosine=jnp.sum(direction*tg,axis=1,keepdims=True)
        rows_of.append(jnp.sum(jnp.where(ii+h*H==jj,cosine,0.0),axis=0,keepdims=True))
        Z[h,0]=(-LOSS_WEIGHT*rinv*(tg-cosine*direction)).astype(BF)
        zc[h].start(); zp[h].start()
    loss(0)
    loss(1)
    cos_o[...]=rows_of[0]+rows_of[1]
    def slope(h):
        zp[h].wait_recv(); zf[h].wait_recv()
        def body(n,c):
            cols=pl.ds(pl.multiple_of(n*256,256),256)
            gs=dot_nt(Z[h].reshape(4*H,C),wo[cols,:])
            y=pre[h,:,cols]
            s=1.0/(1.0+jnp.exp(-y))
            sil[h,:,cols]=(gs*(s*(1.0+y*(1.0-s)))).astype(BF)
            return c
        lax.fori_loop(0,HID//256,body,0)
    def third(h):
        def part(cols):
            y=dot_nt(sil[h],wi[cols,:])
            p2q[h,:,cols]=y[:H]
            p2s[h,1,:,cols]=y[H:2*H].astype(BF)
            p2c[h,:,cols]=y[2*H:3*H]
            p2s[h,0,:,cols]=y[3*H:].astype(BF)
        def body(n,c):
            part(pl.ds(pl.multiple_of(n*256,256),256))
            return c
        lax.fori_loop(0,D//256,body,0)
        if D%256: part(pl.ds(D//256*256,D%256))
        ds[h][0].start(); ds[h][1].start()
    wait_bytes(xh,xsem.at[1])
    xcopy=pltpu.make_async_copy(xh,x_o,osem); xcopy.start()
    scores_prep(xh,kk,vt)
    zc[0].wait_recv(); zf[0].start()
    m=stage(0,xh,kk,vt,sa,None,None,None,None,first=True)
    zc[1].wait_recv(); zf[1].start()
    slope(0); third(0)
    m=pairs(0,1,m)
    pass_on(0,ds,p2c,p2r,p2p)
    slope(1); third(1)
    m=pairs(1,2,m)
    pass_on(1,ds,p2c,p2r,p2p)
    m=pairs(2,5,m)
    loads[2].wait()
    for h in range(2):
        ds[h][1].wait_recv(); ds[h][2].wait_recv()
        rows=pl.ds(h*H,H)
        gh[rows]=(cot[rows].astype(F32)+(p2q[h]+p2r[h,1].astype(F32)+p2r[h,2].astype(F32))).astype(BF)
    R=512
    def heads(i,c):
        at=lax.rem(seq//8+i,L//2//R)
        y=dot_nt(wa[pl.ds(pl.multiple_of(at*R,R),R)],gh[...]).astype(BF)
        gt[pl.ds(at*8,8)]=y.reshape(8,HD,T)
        for e in range(8):
            h=at*8+lax.rem(seq+e,8)
            @pl.when(h!=seq)
            def _():
                remote(gt.at[h],g_o.at[seq],gsem.at[0],gsem.at[1],(dp,h)).start()
            @pl.when(h==seq)
            def _():
                pltpu.make_async_copy(gt.at[h],g_o.at[seq],gsem.at[1]).start()
        return c
    lax.fori_loop(0,4,heads,0)
    m=pairs(5,7,m)
    ucopy(0,0).wait()
    m=stage(NQ-1,xh,kk,vt,sb,sa,m,ua,a_o)
    ucopy(NQ-2,0).start()
    ucopy(0,1).wait()
    stage(NQ,xh,kk,vt,None,sb,m,ub,a_o,last=True)
    ucopy(NQ-1,1).start()
    xcopy.wait()
    for n in range(2): ucopy(n,n).wait()
    for c in hc+hp+hf+zc+zp+zf+cs[0]+cs[1]+ds[0]+ds[1]: c.wait_send()
    wait_bytes(xt.at[pl.ds(0,NB-1)],xsem.at[0])
    wait_bytes(feat.at[pl.ds(0,NB-1)],fsem.at[0])
    wait_bytes(g_o,gsem.at[1]); wait_bytes(gt.at[pl.ds(0,NB-1)],gsem.at[0])


def front(hid,cot,q,k,v,wi,wo,wa,dino):
    vm=pl.BlockSpec(memory_space=pltpu.VMEM); hb=pl.BlockSpec(memory_space=pl.ANY)
    V=pltpu.VMEM; S=pltpu.SemaphoreType.DMA
    return pl.pallas_call(front_kernel,
        in_specs=[vm]*5+[hb]*3+[vm],out_specs=[vm,hb,hb,hb,vm],
        out_shape=[jax.ShapeDtypeStruct((1,T),F32),jax.ShapeDtypeStruct((NB,3*HD,T),BF),jax.ShapeDtypeStruct((NB,HD,T),BF),
            jax.ShapeDtypeStruct((NQ,L,QB),BF),jax.ShapeDtypeStruct((HD+16,L),F32)],
        scratch_shapes=[V((D,HID),BF),V((HID,C),BF),V((2048,D),BF),V((NB,3*HD,T),BF),V((NB,HD,T),BF),V((NB,48,T),BF),
            V((2,4,T//2,D),BF),V((2,4,T//2,C),BF),V((2,2*T,HID),F32),V((2,2*T,HID),BF),
            V((2,2,T//2,C),BF),V((2,T//2,C),F32),V((2,T//2,C),BF),V((2,3,T//2,C),BF),V((2,T//2,C),F32),
            V((2,2,T//2,D),BF),V((2,T//2,D),F32),V((2,T//2,D),BF),V((2,3,T//2,D),BF),V((2,T//2,D),F32),
            V((T,C),F32),V((T,D),BF),
            V((NB,3*HD,T),BF),V((L,T),BF),V((HD+16,L),BF),V((L,QB),F32),V((L,QB),F32),V((L,QB),BF),V((L,QB),BF),
            S((3,)),S((2,)),S((2,)),S((2,)),S((6,)),S((6,)),S((6,)),S((6,)),S((2,3)),S((2,3)),S((2,3)),S((2,3)),S((2,)),S],
        compiler_params=pltpu.CompilerParams(collective_id=0,has_side_effects=True,vmem_limit_bytes=62*2**20),
        name="front")(hid,cot,q,k,v,wi,wo,wa,dino)


def finish_kernel(x_ref,g_ref,a_ref,u_h,buf,vv,kt,ga,qn,gn,rlr,dq,u_ref,o_ref,usem,ksem,qsem):
    dp=lax.axis_index("dp"); seq=lax.axis_index("seq")
    NK=L//KB; per=KB//T
    first=seq//per
    way=1-2*lax.rem(seq,2)
    def place(b): return lax.rem(first+way*(b+1)+2*NK,NK)
    def fetch(b):
        slot=lax.rem(b,2)
        return pltpu.make_async_copy(u_h.at[:,pl.ds(pl.multiple_of(place(b)*KB,KB),KB)],u_ref.at[slot],usem.at[slot])
    fetch(0).start()
    greet(dp,seq,())
    def prep(i):
        grads_prep(i*QP//T,(i+1)*QP//T,x_ref,g_ref,a_ref,vv,kt,ga,qn,gn,rlr)
    def give(h,part,sem):
        @pl.when(h!=seq)
        def _():
            remote(o_ref.at[h,part],buf.at[seq,part],sem.at[0],sem.at[1],(dp,h)).start()
        @pl.when(h==seq)
        def _():
            pltpu.make_async_copy(o_ref.at[h,part],buf.at[seq,part],sem.at[1]).start()
    def block(b,at,v,k,start):
        slot=lax.rem(b,2)
        dk=jnp.zeros((KB,HD),F32); dv=jnp.zeros((KB,HD),F32)
        for i in range(L//QP):
            if start and i+1<L//QP: prep(i+1)
            qr=pl.ds(i*QP,QP)
            n=QP//QB
            u=jnp.concatenate([u_ref[slot,i*n+e] for e in range(n)],axis=1)
            ds=(u.astype(F32)*dot(v,ga[:,qr])).astype(BF)
            dk=dk+dot(ds,qn[qr,:]); dv=dv+dot(u,gn[qr,:])
            part=dot(k,ds)
            if start: dq[:,qr]=part
            else: dq[:,qr]+=part
        for j in range(per):
            o_ref[at*per+j,HD:2*HD]=dk[j*T:(j+1)*T].T.astype(BF)
            o_ref[at*per+j,2*HD:]=dv[j*T:(j+1)*T].T.astype(BF)
        if start: meet(0)
        for j in range(per):
            give(at*per+lax.rem(seq+j,per),pl.ds(HD,2*HD),ksem)
    prep(0)
    at=place(0)
    lane=lax.broadcasted_iota(jnp.int32,(T,HD),1)
    ones=jnp.where(lane<2,1.0,0.0).astype(BF)
    v=jnp.concatenate([jnp.concatenate([x_ref[at*per+j,2*HD:].T,ones],axis=1) for j in range(per)],axis=0)
    k=jnp.concatenate([x_ref[at*per+j,HD:2*HD]*BF(0.125) for j in range(per)],axis=1)
    fetch(1).start()
    fetch(0).wait()
    block(0,at,v,k,True)
    def body(b,c):
        @pl.when(b<NK-1)
        def _(): fetch(b+1).start()
        fetch(b).wait()
        at=place(b)
        kr=pl.ds(pl.multiple_of(at*KB,KB),KB)
        block(b,at,vv[kr,:],kt[:,kr],False)
        return c
    lax.fori_loop(1,NK,body,0)
    for j in range(NB):
        o_ref[j,:HD]=(dq[:,j*T:(j+1)*T]*rlr[0:1,j*T:(j+1)*T]).astype(BF)
    def send(r,c):
        give(lax.rem(seq+r,NB),pl.ds(0,HD),qsem)
        return c
    lax.fori_loop(0,NB,send,0)
    wait_bytes(buf.at[:,pl.ds(HD,2*HD)],ksem.at[1])
    wait_bytes(buf.at[:,pl.ds(0,HD)],qsem.at[1])
    wait_bytes(buf.at[pl.ds(0,NB-1),pl.ds(HD,2*HD)],ksem.at[0])
    wait_bytes(buf.at[pl.ds(0,NB-1),pl.ds(0,HD)],qsem.at[0])


def finish(x,g,u,a):
    V=pltpu.VMEM; S=pltpu.SemaphoreType.DMA
    vm=pl.BlockSpec(memory_space=V); hb=pl.BlockSpec(memory_space=pl.ANY)
    return pl.pallas_call(finish_kernel,in_specs=[vm]*3+[hb],out_specs=vm,
        out_shape=jax.ShapeDtypeStruct((NB,3*HD,T),BF),
        scratch_shapes=[V((L,T),BF),V((HD,L),BF),V((T,L),BF),V((L,HD),BF),V((L,HD),BF),V((8,L),F32),V((HD,L),F32),
            V((2,NQ,KB,QB),BF),V((NB,3*HD,T),BF),S((2,)),S((2,)),S((2,))],
        compiler_params=pltpu.CompilerParams(collective_id=1,has_side_effects=True,vmem_limit_bytes=56*2**20),
        name="finish")(x,g,a,u)


def place_kernel(o_ref,q_o,k_o,v_o):
    for n,ref in enumerate((q_o,k_o,v_o)):
        for p in range(o_ref.shape[0]//2):
            ref[:,p*T:(p+1)*T]=o_ref[2*p:2*p+2,n*HD:(n+1)*HD].reshape(T,T).T


def place(o):
    steps=2
    return pl.pallas_call(place_kernel,grid=(steps,),
        in_specs=[pl.BlockSpec((NB//steps,3*HD,T),lambda i:(i,0,0))],
        out_specs=[pl.BlockSpec((T,NB*HD//steps),lambda i:(0,i))]*3,
        out_shape=[jax.ShapeDtypeStruct((T,NB*HD),BF)]*3,name="place")(o)


def on_device(hidden,out_cot,proj_in,proj_out,attn_out_w,queries,keys,values,dino):
    cosine,x,g,u,a=front(hidden[0],out_cot[0],queries[0],keys[0],values[0],proj_in,proj_out,attn_out_w,dino[0])
    gq,gk,gv=place(finish(x,g,u,a))
    return cosine,gq[None],gk[None],gv[None]


def solution(mesh):
    in_specs = (
        P("dp", "seq", None),
        P("dp", "seq", None),
        P(None, "dp"),
        P("dp", None),
        P(),
        P("dp", "seq", None),
        P("dp", "seq", None),
        P("dp", "seq", None),
        P("dp", "seq", None),
    )
    out_specs = (P("dp", "seq"), P("dp", "seq", None), P("dp", "seq", None), P("dp", "seq", None))
    return jax.shard_map(
        on_device, mesh=mesh, in_specs=in_specs, out_specs=out_specs, check_vma=False
    )
```
